256 devices in a mesh: dp: 32 (over x_lo, z, core), tensor: 8 (over y, x_hi).
Axes of the slice: x: 4 (x_hi: 2, x_lo: 2; x = x_hi * 2 + x_lo), y: 4, z: 8, core: 2. Of those that a mesh axis runs over, the one named last changes fastest.
Arguments:
- images: bfloat16 [4096, 1152], P('dp'), may hold values from -6 to 6
- gain: float32 [1152], replicated, may hold values from 0.1 to 1.9
- w_in: bfloat16 [1152, 4304], P(None, 'tensor'), may hold values from -0.1875 to 0.1875
- b_in: float32 [4304], P('tensor'), may hold values from -4 to 4
- w_out: bfloat16 [4304, 1152], P('tensor'), may hold values from -0.09375 to 0.09375
- texts: bfloat16 [4096, 1152], P(('dp', 'tensor')), may hold values from -6 to 6
- log_scale: float32 [1], replicated, may hold values from 1.6 to 3
- bias: float32 [1], replicated, may hold values from -3 to -0.5
Outputs:
- image_loss_gradient: float32 [4096, 1152], P('dp')
- text_grad: float32 [4096, 1152], P(('dp', 'tensor'))
- in_grad: float32 [1152, 4304], P('dp', 'tensor')
- out_grad_t: float32 [1152, 4304], P('dp', 'tensor')
The draws below stay inside these ranges and needn't reach their ends.
All inputs are finite; a program needn't handle non-finite values.
Results may differ from the reference program's by a relative error of at most 0.019.
Values may be sent and summed in bfloat16 or wider, within the bound.
No kernel may reach another device: no remote copies, remote signals or barrier semaphores. Data moves between devices by JAX's collectives and lax.ppermute only.
A program may use at most 64 MiB of HBM per device.

```python
import jax
import jax.numpy as jnp
from jax import lax

D = 1152
FF = 4304
IMG_DEV = 128
BATCH = 4096


def shard_levels(own_key, extent, pieces, low, top_value):
    level, own = 1.0, jax.random.fold_in(own_key, 6)
    for axis_at, blocks in pieces:
        draws = jnp.exp(jax.random.uniform(jax.random.fold_in(own, axis_at), (blocks,), jnp.float32, low / len(pieces), top_value / len(pieces)))
        level = level * jnp.repeat(draws, extent[axis_at] // blocks).reshape([-1 if axis == axis_at else 1 for axis in range(len(extent))])
    return level


def scatter_about(rng, shape, width, bound, split=(), kind=jnp.bfloat16):
    entries = jax.random.normal(rng, shape, jnp.float32) * width
    if len(split) > 0:
        entries = shard_levels(rng, shape, split, -0.22, 0.18) * entries
    return jnp.clip(entries, min=-bound, max=bound).astype(kind)


def setup_inputs(seed: int = 0) -> dict:
    keys = jax.random.split(jax.random.key(seed), 9)
    images = scatter_about(keys[0], (BATCH, D), 1.0, 6.0, ((0, 32),))
    gain = jnp.clip(1.0 + 0.18 * jax.random.normal(keys[1], (D,), jnp.float32), 0.1, 1.9)
    w_in = scatter_about(keys[2], (D, FF), D ** -0.5, 0.1875, ((1, 8),))
    b_in = scatter_about(keys[3], (FF,), 0.7, 4.0, ((0, 8),), jnp.float32)
    w_out = scatter_about(keys[4], (FF, D), FF ** -0.5, 0.09375, ((0, 8),))
    texts = scatter_about(keys[5], (BATCH, D), 1.0, 6.0, ((0, 256),))
    log_scale = jnp.clip(jax.random.uniform(keys[6], (1,), jnp.float32, 1.6, 3.0), 1.6, 3.0)
    bias = jnp.clip(jax.random.uniform(keys[7], (1,), jnp.float32, -3.0, -0.5), -3.0, -0.5)
    return {"images": images, "gain": gain, "w_in": w_in, "b_in": b_in, "w_out": w_out, "texts": texts, "log_scale": log_scale, "bias": bias}


def gelu_tanh(value):
    return jax.nn.gelu(value, approximate=True)

def reference(images, gain, w_in, b_in, w_out, texts, log_scale, bias):
    xf = images.astype(jnp.float32)
    feature_average = lax.optimization_barrier(jnp.mean(xf, axis=-1, keepdims=True))
    centered_input = xf - feature_average
    standard_deviation = jnp.sqrt(lax.optimization_barrier(jnp.mean(centered_input * centered_input, axis=-1, keepdims=True)) + 1e-06)
    standardized_input = centered_input / standard_deviation
    normalized_rows = (standardized_input * gain).astype(jnp.bfloat16)
    pre = jnp.dot(normalized_rows, w_in, preferred_element_type=jnp.float32) + b_in
    hidden = gelu_tanh(pre).astype(jnp.bfloat16)
    embed = xf + jnp.dot(hidden, w_out, preferred_element_type=jnp.float32)
    enorm = jnp.sqrt(lax.optimization_barrier(jnp.sum(embed * embed, axis=-1, keepdims=True)) + 1e-06)
    unit = embed / enorm
    unit_b = unit.astype(jnp.bfloat16)
    tf = texts.astype(jnp.float32)
    tnorm = jnp.sqrt(lax.optimization_barrier(jnp.sum(tf * tf, axis=-1, keepdims=True)) + 1e-06)
    tunit = tf / tnorm
    tunit_b = tunit.astype(jnp.bfloat16)
    scale = jnp.exp(log_scale[0])
    shift = bias[0]
    columns = jnp.arange(BATCH, dtype=jnp.int32)
    blocks = BATCH // IMG_DEV

    def block_step(total, index):
        first = (index * IMG_DEV).astype(jnp.int32)
        rows_b = lax.dynamic_slice_in_dim(unit_b, first, IMG_DEV, 0)
        logits = scale * lax.dot_general(rows_b, tunit_b, (((1,), (1,)), ((), ())), preferred_element_type=jnp.float32) + shift
        labels = ((first + jnp.arange(IMG_DEV, dtype=jnp.int32))[:, None] == columns[None, :]).astype(jnp.float32)
        coef = (jax.nn.sigmoid(logits) - labels).astype(jnp.bfloat16)
        du_block = scale * jnp.dot(coef, tunit_b, preferred_element_type=jnp.float32)
        total = total + scale * lax.dot_general(coef, rows_b, (((0,), (0,)), ((), ())), preferred_element_type=jnp.float32)
        return (total, du_block)
    dw, du_blocks = lax.scan(block_step, jnp.zeros((BATCH, D), jnp.float32), jnp.arange(blocks, dtype=jnp.int32))
    du = du_blocks.reshape(BATCH, D)
    text_grad = (dw - tunit * lax.optimization_barrier(jnp.sum(tunit * dw, axis=-1, keepdims=True))) / tnorm
    embedding_gradient = ((du - unit * lax.optimization_barrier(jnp.sum(unit * du, axis=-1, keepdims=True))) / enorm).astype(jnp.bfloat16)
    dhid = lax.dot_general(embedding_gradient, w_out, (((1,), (1,)), ((), ())), preferred_element_type=jnp.float32)
    unused, pull = jax.vjp(gelu_tanh, pre)
    dpre = pull(dhid)[0].astype(jnp.bfloat16)
    dn = lax.dot_general(dpre, w_in, (((1,), (1,)), ((), ())), preferred_element_type=jnp.float32)
    unit_input_gradient = dn * gain
    image_loss_gradient = embedding_gradient.astype(jnp.float32) + (unit_input_gradient - lax.optimization_barrier(jnp.mean(unit_input_gradient, axis=-1, keepdims=True)) - standardized_input * lax.optimization_barrier(jnp.mean(unit_input_gradient * standardized_input, axis=-1, keepdims=True))) / standard_deviation
    in_grad = lax.dot_general(normalized_rows, dpre, (((0,), (0,)), ((), ())), preferred_element_type=jnp.float32)
    out_grad_t = lax.dot_general(embedding_gradient, hidden, (((0,), (0,)), ((), ())), preferred_element_type=jnp.float32)
    return (image_loss_gradient, text_grad, in_grad, out_grad_t)
```

```python
import jax
import jax.numpy as jnp
from jax import lax
from jax.experimental import pallas as pl
from jax.experimental.pallas import tpu as pltpu
from jax.sharding import PartitionSpec as P

F32 = jnp.float32
BF = jnp.bfloat16
I32 = jnp.int32
D = 1152
FF_T = 538
NT = 8
ROWS = 16
COLS = 36
IMG = 128
SEL = 320
LANES = 640
OUT_AT = 576
ROOT = 0.7978845608028654


def dot(a, b, ca=1, cb=0):
    return lax.dot_general(a, b, (((ca,), (cb,)), ((), ())), preferred_element_type=F32)


def swap(x, axis, n, mask):
    return lax.ppermute(x, axis, [(i, i ^ mask) for i in range(n)])


def sds(shape, dtype):
    return jax.ShapeDtypeStruct(shape, dtype)


def hold(x):
    return pltpu.with_memory_space_constraint(x, pltpu.HBM)


def call(body, outs, args, scratch=(), smem=(), after=(), hbm=(), flops=0, size=1 << 20):
    single = not isinstance(outs, (tuple, list))
    outs = (outs,) if single else tuple(outs)
    vm = pl.BlockSpec(memory_space=pltpu.VMEM)
    sm = pl.BlockSpec(memory_space=pltpu.SMEM)
    some = pl.BlockSpec(memory_space=pl.ANY)
    far = pl.BlockSpec(memory_space=pltpu.HBM)
    n_in, n_after, n_out, n_far = len(args), len(after), len(outs), len(hbm)

    def kernel(*refs):
        ins = refs[:n_in]
        results = list(refs[n_in + n_after : n_in + n_after + n_out])
        rest = refs[n_in + n_after + n_out :]
        near, sems, own = rest[:n_far], rest[n_far : 2 * n_far], rest[2 * n_far :]
        copies = []
        for ref, at, sem in zip(near, hbm, sems):
            copies.append(pltpu.make_async_copy(ref, results[at], sem))
            results[at] = ref
        body(*ins, *results, *own)
        for copy in copies:
            copy.start()
        for copy in copies:
            copy.wait()

    got = pl.pallas_call(
        kernel,
        out_shape=tuple(
            pltpu.HBM(o.shape, o.dtype) if i in hbm else o for i, o in enumerate(outs)
        ),
        in_specs=[sm if i in smem else vm for i in range(n_in)] + [some] * n_after,
        out_specs=tuple(far if i in hbm else vm for i in range(n_out)),
        scratch_shapes=[pltpu.VMEM(outs[i].shape, outs[i].dtype) for i in hbm]
        + [pltpu.SemaphoreType.DMA(()) for _ in hbm]
        + list(scratch),
        compiler_params=pltpu.CompilerParams(vmem_limit_bytes=24 << 20),
        cost_estimate=pl.CostEstimate(flops=flops, bytes_accessed=size, transcendentals=0),
    )(*args, *[hold(x) for x in after])
    return got[0] if single else got


def text_unit(tf):
    tnorm = jnp.sqrt(jnp.sum(tf * tf, axis=-1, keepdims=True) + 1e-06)
    return tf / tnorm, tnorm


def text_body(mine, *refs):
    out = refs[3]
    for k, ref in enumerate((mine,) + refs[:3]):
        out[k] = text_unit(ref[...].astype(F32))[0].astype(BF)


def layer_stats(xf):
    centered = xf - jnp.mean(xf, axis=-1, keepdims=True)
    sd = jnp.sqrt(jnp.mean(centered * centered, axis=-1, keepdims=True) + 1e-06)
    return centered / sd, sd


def forward_body(images, gain, w_in, b_in, w_out, normed, hidden, slope, part, *scratch):
    v_images, v_in, v_out, v_normed, v_hidden, v_slope, v_part, sem = scratch

    def move(src, dst, k):
        copy = pltpu.make_async_copy(src, dst, sem.at[k])
        copy.start()
        return copy

    get_images = move(images, v_images, 0)
    get_in = move(w_in, v_in, 1)
    get_out = move(w_out, v_out, 2)
    get_images.wait()
    xhat, _ = layer_stats(v_images[...].astype(F32))
    normed_b = (xhat * gain[...].reshape(1, D)).astype(BF)
    v_normed[...] = normed_b
    put_normed = move(v_normed, normed, 3)
    get_in.wait()
    pre = dot(normed_b, v_in[...], 1, 1) + b_in[...].reshape(1, FF_T)
    square = pre * pre
    th = jnp.tanh(ROOT * (pre + 0.044715 * (square * pre)))
    cdf = 0.5 * (1.0 + th)
    hidden_b = (pre * cdf).astype(BF)
    v_hidden[...] = hidden_b
    put_hidden = move(v_hidden, hidden, 4)
    get_out.wait()
    v_part[...] = dot(hidden_b, v_out[...]).astype(BF).reshape(NT, ROWS, D)
    put_part = move(v_part, part, 5)
    v_slope[...] = cdf + 0.5 * pre * (1.0 - th * th) * (ROOT * (1.0 + 0.134145 * square))
    put_slope = move(v_slope, slope, 6)
    for copy in (put_normed, put_hidden, put_part, put_slope):
        copy.wait()


def forward(images, gain, w_in, b_in, w_out):
    far = pl.BlockSpec(memory_space=pltpu.HBM)
    near = pl.BlockSpec(memory_space=pltpu.VMEM)

    shapes = (
        ((IMG, D), BF),
        ((IMG, FF_T), BF),
        ((IMG, FF_T), F32),
        ((NT, ROWS, D), BF),
    )
    return pl.pallas_call(
        forward_body,
        out_shape=tuple(pltpu.HBM(*shape) for shape in shapes),
        in_specs=[far, near, far, near, far],
        out_specs=(far,) * 4,
        scratch_shapes=[
            pltpu.VMEM((IMG, D), BF),
            pltpu.VMEM((FF_T, D), BF),
            pltpu.VMEM((FF_T, D), BF),
        ]
        + [pltpu.VMEM(*shape) for shape in shapes]
        + [pltpu.SemaphoreType.DMA((7,))],
        compiler_params=pltpu.CompilerParams(vmem_limit_bytes=24 << 20),
        cost_estimate=pl.CostEstimate(
            flops=2 * 160_000_000, bytes_accessed=4 << 20, transcendentals=0
        ),
    )(hold(images), hold(gain), hold(w_in), hold(b_in), hold(w_out))


def embed_body(rank, images, got, t_a, t_b, t_c, t_d, unit, enorm, spread, four):
    text_body(t_a, t_b, t_c, t_d, four)
    at = pl.multiple_of(rank[0] * ROWS, ROWS)
    embed = images[pl.ds(at, ROWS), :].astype(F32)
    embed = embed + jnp.sum(got[...].astype(F32), axis=0)
    norm = jnp.sqrt(jnp.sum(embed * embed, axis=-1, keepdims=True) + 1e-06)
    value = embed / norm
    unit[...] = value
    enorm[...] = jnp.broadcast_to(norm, (ROWS, 128))
    value = value.astype(BF)
    for k in range(NT):
        spread[k] = value


def pairs_body(rank, log_scale, bias, unit, *refs):
    du, c_own, c_oth = refs[8:]
    scale = jnp.exp(jnp.full((1, 1), log_scale[0], F32))
    u = unit[...].reshape(IMG, D)
    total = None
    for half, out in ((0, c_own), (4, c_oth)):
        texts = jnp.concatenate([ref[...].reshape(64, D) for ref in refs[half : half + 4]], axis=0)
        coef = jax.nn.sigmoid(scale * dot(u, texts, 1, 1) + bias[0])
        if half == 0:
            row = lax.broadcasted_iota(I32, (IMG, 256), 0) - rank[0] * ROWS
            col = lax.broadcasted_iota(I32, (IMG, 256), 1)
            coef = coef - jnp.where((row == col) & (col < ROWS), 1.0, 0.0)
        coef = coef.astype(BF)
        out[...] = coef
        part = dot(coef, texts)
        total = part if half == 0 else total + part
    du[...] = (scale * total).astype(BF).reshape(NT, ROWS, D)


def text_grad_body(log_scale, c_mine, u_mine, c_got, u_got, keep, *sent):
    scale = jnp.exp(jnp.full((1, 1), log_scale[0], F32))
    dw = dot(c_mine[...], u_mine[...].reshape(IMG, D), 0, 0)
    dw = scale * (dw + dot(c_got[...], u_got[...].reshape(IMG, D), 0, 0))
    keep[...] = dw[:64]
    for k in range(3):
        sent[k][...] = dw[64 * (k + 1) : 64 * (k + 2)].astype(BF)


def text_fold_body(keep, a, b, c, rest, *sent):
    dw = keep[...] + a[...].astype(F32) + b[...].astype(F32) + c[...].astype(F32)
    rest[...] = dw[:ROWS]
    for k in range(3):
        sent[k][...] = dw[ROWS * (k + 1) : ROWS * (k + 2)].astype(BF)


def embed_grad_body(got, unit, enorm, rows, spread):
    du = jnp.sum(got[...].astype(F32), axis=0)
    u = unit[...]
    de = (du - u * jnp.sum(u * du, axis=-1, keepdims=True)) / enorm[:, :1]
    de = de.astype(BF)
    rows[...] = de
    for k in range(NT):
        spread[k] = de


def slope_body(rank, de, w_out, slope, dpre, *sent):
    value = dot(de[...].reshape(IMG, D), w_out[...], 1, 1) * slope[...]
    dpre[...] = value.astype(BF)
    pack_body(rank, de, dpre, *sent)


def dn_body(dpre, w_in, keep, t_a, t_b, t_c, dn, rest, *sent):
    dn[...] = dot(dpre[...], w_in[...]).astype(BF).reshape(NT, ROWS, D)
    text_fold_body(keep, t_a, t_b, t_c, rest, *sent)


def pack(rank, left, right, lefts, rights):
    r = lax.broadcasted_iota(I32, (SEL, 1), 0)
    block = (r * 52429) >> 21
    place = r - block * 40
    base = jnp.where(place < COLS, block * 72 + place, -4096)
    diff = lax.broadcasted_iota(I32, (SEL, LANES), 1) - base
    for ref, at, x_flip, c_flip in lefts:
        x, c = rank[2] ^ x_flip, rank[1] ^ c_flip
        window = pl.ds(pl.multiple_of(x * 512, 512), LANES)
        one = jnp.where(diff == x * 64 + c * COLS, 1.0, 0.0).astype(BF)
        ref[at : at + SEL] = dot(one, left[:, :, window].reshape(IMG, LANES), 1, 1).astype(BF)
    wide = jnp.concatenate([right[...].astype(F32), jnp.zeros((IMG, LANES - FF_T), F32)], axis=1)
    wide = wide.astype(BF)
    for k in range(5):
        for ref, at in rights:
            ref[at + k * 128 : at + (k + 1) * 128] = wide[:, k * 128 : (k + 1) * 128]


def pack_relay_body(rank, left, right, mine, to_core, to_x):
    lefts = ((mine, 0, 0, 0), (to_core, 0, 0, 1), (to_x, 0, 1, 0), (to_x, SEL, 1, 1))
    pack(rank, left, right, lefts, ((to_core, SEL), (to_x, 2 * SEL)))


def pack_body(rank, left, right, mine, to_core, to_x, to_both):
    lefts = ((to_x, 0, 1, 0), (to_both, 0, 1, 1), (mine, 0, 0, 0), (to_core, 0, 0, 1))
    pack(rank, left, right, lefts, ((to_core, SEL), (to_x, SEL), (to_both, SEL)))


def weights_body(*refs):
    n_mine, n_own, n_core, n_x, n_xc = refs[:5]
    e_mine, e_own, e_core, e_x, e_xc = refs[5:10]
    out = refs[10]

    def left(*parts):
        return jnp.concatenate([ref[at : at + SEL] for ref, at in parts], axis=1)

    def right(*parts):
        rows = []
        for ref, at in parts:
            chunks = [ref[at + k * 128 : at + (k + 1) * 128] for k in range(5)]
            rows.append(jnp.concatenate(chunks, axis=1))
        return jnp.concatenate(rows, axis=0)

    in_part = dot(
        left((n_mine, 0), (n_core, 0), (n_x, 0), (n_xc, SEL)),
        right((e_own, SEL), (e_core, SEL), (e_x, SEL), (e_xc, SEL)),
    )
    out_part = dot(
        left((e_mine, 0), (e_core, 0), (e_x, 0), (e_xc, 0)),
        right((n_own, SEL), (n_core, SEL), (n_x, 2 * SEL), (n_xc, 2 * SEL)),
    )
    both = jnp.concatenate([in_part[:, :OUT_AT], out_part[:, :OUT_AT]], axis=1)
    for k in range(8):
        out[k] = both[k * 40 : (k + 1) * 40].astype(BF)


def image_body(rank, got, images, gain, de_rows, rows):
    dn = jnp.sum(got[...].astype(F32), axis=0)
    at = pl.multiple_of(rank[0] * ROWS, ROWS)
    xhat, sd = layer_stats(images[pl.ds(at, ROWS), :].astype(F32))
    dxh = dn * gain[...].reshape(1, D)
    grad = (
        dxh
        - jnp.mean(dxh, axis=-1, keepdims=True)
        - xhat * jnp.mean(dxh * xhat, axis=-1, keepdims=True)
    ) / sd
    rows[...] = (de_rows[...].astype(F32) + grad).astype(BF)


def place_body(rank, *refs):
    out = refs[NT]
    for ref, k in zip(refs[:NT], (0, 1, 2, 4, 6, 3, 5, 7)):
        at = pl.multiple_of((rank[0] ^ k) * ROWS, ROWS)
        out[pl.ds(at, ROWS), :] = ref[...].astype(F32)


def final_body(got, texts, rest, a, b, c, text_grad, in_grad, out_grad):
    total = got[0].astype(F32)
    for k in range(1, 8):
        total = total + got[k].astype(F32)
    in_grad[...] = total[:COLS, 0:FF_T]
    out_grad[...] = total[:COLS, OUT_AT : OUT_AT + FF_T]
    dw = rest[...] + a[...].astype(F32) + b[...].astype(F32) + c[...].astype(F32)
    tunit, tnorm = text_unit(texts[...].astype(F32))
    text_grad[...] = (dw - tunit * jnp.sum(tunit * dw, axis=-1, keepdims=True)) / tnorm


def local(images, gain, w_in, b_in, w_out, texts, log_scale, bias):
    rank_d = lax.axis_index("dp")
    rank_t = lax.axis_index("tensor")
    rank = jnp.stack([rank_t, rank_d % 2, rank_d // 16]).astype(I32)
    w_in = w_in.T
    block = sds((ROWS, D), BF)
    blocks = sds((NT, ROWS, D), BF)
    groups = [[x * 16 + k * 2 + c for k in range(8)] for x in range(2) for c in range(2)]

    def tensor_all(x):
        return lax.all_to_all(x, "tensor", 0, 0, tiled=True)

    def dp(x, mask):
        return swap(x, "dp", 32, mask)

    normed, hidden, slope, part = forward(images, gain, w_in, b_in, w_out)
    unit, enorm, spread, four = call(
        embed_body,
        (sds((ROWS, D), F32), sds((ROWS, 128), F32), blocks, sds((4, ROWS, D), BF)),
        (rank, hold(images), tensor_all(part), hold(texts), dp(texts, 4), dp(texts, 8), dp(texts, 12)),
        smem=(0,),
        hbm=(0, 1, 2, 3),
    )
    t_own = [four, dp(four, 2), dp(four, 16), dp(four, 18)]
    t_oth = [dp(x, 1) for x in t_own]
    unit_b = tensor_all(spread)
    du, c_own, c_oth = call(
        pairs_body,
        (blocks, sds((IMG, 256), BF), sds((IMG, 256), BF)),
        (rank, log_scale, bias, unit_b, hold(four), *t_own[1:], *t_oth),
        smem=(0, 1, 2),
        hbm=(0, 1, 2),
        flops=2 * 150_000_000,
        size=2 << 20,
    )
    u_got = dp(unit_b, 1)
    c_got = dp(c_oth, 1)
    sixty = sds((4 * ROWS, D), BF)
    keep, *sent = call(
        text_grad_body,
        (sds((4 * ROWS, D), F32), sixty, sixty, sixty),
        (log_scale, hold(c_own), unit_b, c_got, u_got),
        smem=(0,),
        hbm=(0, 1, 2, 3),
        flops=2 * 75_000_000,
        size=2 << 20,
    )
    got = [dp(x, mask) for x, mask in zip(sent, (2, 16, 18))]
    n_mine, n_own, n_tox = call(
        pack_relay_body,
        (sds((SEL, 128), BF), sds((3 * SEL, 128), BF), sds((4 * SEL, 128), BF)),
        (rank, hold(normed.reshape(NT, ROWS, D)), hold(hidden)),
        smem=(0,),
        hbm=(0, 1, 2),
        after=(du,),
        flops=2 * 100_000_000,
        size=2 << 20,
    )
    n_core = dp(n_own, 1)
    n_x = dp(n_tox, 16)
    n_xc = dp(n_x, 1)
    de_rows, spread = call(
        embed_grad_body,
        (block, blocks),
        (tensor_all(du), hold(unit), hold(enorm)),
        hbm=(0, 1),
        after=(keep, n_own),
    )
    de = tensor_all(spread)

    operand = sds((3 * SEL, 128), BF)
    dpre, e_mine, e_own, e_tox, e_toxc = call(
        slope_body,
        (sds((IMG, FF_T), BF), sds((SEL, 128), BF), operand, operand, operand),
        (rank, de, hold(w_out), hold(slope)),
        smem=(0,),
        hbm=(1, 2, 3, 4),
        after=(n_x,),
        flops=2 * 180_000_000,
        size=4 << 20,
    )
    e_x = dp(e_tox, 16)
    e_xc = dp(e_toxc, 17)
    e_core = dp(e_own, 1)
    dn, rest, *sent = call(
        dn_body,
        (blocks, sds((ROWS, D), F32), block, block, block),
        (dpre, w_in, hold(keep), *got),
        hbm=(0, 1, 2, 3, 4),
        after=(n_core, n_xc),
        flops=2 * 80_000_000,
        size=2 << 20,
    )
    dn = tensor_all(dn)
    got = [dp(x, mask) for x, mask in zip(sent, (4, 8, 12))]
    rows = call(
        image_body, block, (rank, dn, hold(images), hold(gain), hold(de_rows)), smem=(0,), hbm=(0,)
    )
    payload = call(
        weights_body,
        sds((8, 40, D), BF),
        (hold(n_mine), hold(n_own), n_core, n_x, n_xc)
        + (hold(e_mine), hold(e_own), e_core, e_x, e_xc),
        hbm=(0,),
        after=(rows, *got),
        flops=2 * 160_000_000,
        size=3 << 20,
    )
    total = lax.all_to_all(payload, "dp", 0, 0, tiled=True, axis_index_groups=groups)

    spread = [rows] + [swap(rows, "tensor", NT, k) for k in (1, 2, 4, 6)]
    spread += [swap(spread[1], "tensor", NT, k) for k in (2, 4, 6)]
    image_grad = call(place_body, sds((IMG, D), F32), (rank, *spread), smem=(0,))
    text_grad, in_grad, out_grad = call(
        final_body,
        (sds((ROWS, D), F32), sds((COLS, FF_T), F32), sds((COLS, FF_T), F32)),
        (total, hold(texts), hold(rest), *got),
    )
    return (image_grad, text_grad, in_grad, out_grad)


def solution(mesh):
    return jax.shard_map(
        local,
        mesh=mesh,
        in_specs=(
            P("dp", None),
            P(),
            P(None, "tensor"),
            P("tensor"),
            P("tensor", None),
            P(("dp", "tensor"), None),
            P(),
            P(),
        ),
        out_specs=(P("dp", None), P(("dp", "tensor"), None), P("dp", "tensor"), P("dp", "tensor")),
        check_vma=False,
    )
```

```python
import jax
import jax.numpy as jnp
from jax import lax
from jax.experimental import pallas as pl
from jax.experimental.pallas import tpu as pltpu
from jax.sharding import PartitionSpec as P

F32 = jnp.float32
BF = jnp.bfloat16
I32 = jnp.int32
D = 1152
FF_T = 538
NT = 8
ROWS = 16
COLS = 36
IMG = 128
SEL = 320
LANES = 640
OUT_AT = 576
ROOT = 0.7978845608028654


def dot(a, b, ca=1, cb=0):
    return lax.dot_general(a, b, (((ca,), (cb,)), ((), ())), preferred_element_type=F32)


def swap(x, axis, n, mask):
    return lax.ppermute(x, axis, [(i, i ^ mask) for i in range(n)])


def sds(shape, dtype):
    return jax.ShapeDtypeStruct(shape, dtype)


def hold(x):
    return pltpu.with_memory_space_constraint(x, pltpu.HBM)


def call(body, outs, args, scratch=(), smem=(), after=(), hbm=(), flops=0, size=1 << 20):
    single = not isinstance(outs, (tuple, list))
    outs = (outs,) if single else tuple(outs)
    vm = pl.BlockSpec(memory_space=pltpu.VMEM)
    sm = pl.BlockSpec(memory_space=pltpu.SMEM)
    some = pl.BlockSpec(memory_space=pl.ANY)
    far = pl.BlockSpec(memory_space=pltpu.HBM)
    n_in, n_after, n_out, n_far = len(args), len(after), len(outs), len(hbm)

    def kernel(*refs):
        ins = refs[:n_in]
        results = list(refs[n_in + n_after : n_in + n_after + n_out])
        rest = refs[n_in + n_after + n_out :]
        near, sems, own = rest[:n_far], rest[n_far : 2 * n_far], rest[2 * n_far :]
        copies = []
        for ref, at, sem in zip(near, hbm, sems):
            copies.append(pltpu.make_async_copy(ref, results[at], sem))
            results[at] = ref
        body(*ins, *results, *own)
        for copy in copies:
            copy.start()
        for copy in copies:
            copy.wait()

    got = pl.pallas_call(
        kernel,
        out_shape=tuple(
            pltpu.HBM(o.shape, o.dtype) if i in hbm else o for i, o in enumerate(outs)
        ),
        in_specs=[sm if i in smem else vm for i in range(n_in)] + [some] * n_after,
        out_specs=tuple(far if i in hbm else vm for i in range(n_out)),
        scratch_shapes=[pltpu.VMEM(outs[i].shape, outs[i].dtype) for i in hbm]
        + [pltpu.SemaphoreType.DMA(()) for _ in hbm]
        + list(scratch),
        compiler_params=pltpu.CompilerParams(vmem_limit_bytes=24 << 20),
        cost_estimate=pl.CostEstimate(flops=flops, bytes_accessed=size, transcendentals=0),
    )(*args, *[hold(x) for x in after])
    return got[0] if single else got


def text_unit(tf):
    tnorm = jnp.sqrt(jnp.sum(tf * tf, axis=-1, keepdims=True) + 1e-06)
    return tf / tnorm, tnorm


def text_body(mine, *refs):
    out = refs[3]
    for k, ref in enumerate((mine,) + refs[:3]):
        out[k] = text_unit(ref[...].astype(F32))[0].astype(BF)


def layer_stats(xf):
    centered = xf - jnp.mean(xf, axis=-1, keepdims=True)
    sd = jnp.sqrt(jnp.mean(centered * centered, axis=-1, keepdims=True) + 1e-06)
    return centered / sd, sd


def forward_body(images, gain, w_in, b_in, w_out, normed, hidden, slope, part, *scratch):
    v_images, v_in, v_out, v_normed, v_hidden, v_slope, v_part, sem = scratch

    def move(src, dst, k):
        copy = pltpu.make_async_copy(src, dst, sem.at[k])
        copy.start()
        return copy

    get_images = move(images, v_images, 0)
    get_in = move(w_in, v_in, 1)
    get_out = move(w_out, v_out, 2)
    get_images.wait()
    xhat, _ = layer_stats(v_images[...].astype(F32))
    normed_b = (xhat * gain[...].reshape(1, D)).astype(BF)
    v_normed[...] = normed_b
    put_normed = move(v_normed, normed, 3)
    get_in.wait()
    pre = dot(normed_b, v_in[...], 1, 1) + b_in[...].reshape(1, FF_T)
    square = pre * pre
    th = jnp.tanh(ROOT * (pre + 0.044715 * (square * pre)))
    cdf = 0.5 * (1.0 + th)
    hidden_b = (pre * cdf).astype(BF)
    v_hidden[...] = hidden_b
    put_hidden = move(v_hidden, hidden, 4)
    get_out.wait()
    v_part[...] = dot(hidden_b, v_out[...]).astype(BF).reshape(NT, ROWS, D)
    put_part = move(v_part, part, 5)
    v_slope[...] = cdf + 0.5 * pre * (1.0 - th * th) * (ROOT * (1.0 + 0.134145 * square))
    put_slope = move(v_slope, slope, 6)
    for copy in (put_normed, put_hidden, put_part, put_slope):
        copy.wait()


def forward(images, gain, w_in, b_in, w_out):
    far = pl.BlockSpec(memory_space=pltpu.HBM)
    near = pl.BlockSpec(memory_space=pltpu.VMEM)

    shapes = (
        ((IMG, D), BF),
        ((IMG, FF_T), BF),
        ((IMG, FF_T), F32),
        ((NT, ROWS, D), BF),
    )
    return pl.pallas_call(
        forward_body,
        out_shape=tuple(pltpu.HBM(*shape) for shape in shapes),
        in_specs=[far, near, far, near, far],
        out_specs=(far,) * 4,
        scratch_shapes=[
            pltpu.VMEM((IMG, D), BF),
            pltpu.VMEM((FF_T, D), BF),
            pltpu.VMEM((FF_T, D), BF),
        ]
        + [pltpu.VMEM(*shape) for shape in shapes]
        + [pltpu.SemaphoreType.DMA((7,))],
        compiler_params=pltpu.CompilerParams(vmem_limit_bytes=24 << 20),
        cost_estimate=pl.CostEstimate(
            flops=2 * 160_000_000, bytes_accessed=4 << 20, transcendentals=0
        ),
    )(hold(images), hold(gain), hold(w_in), hold(b_in), hold(w_out))


def embed_body(rank, images, got, t_a, t_b, t_c, t_d, unit, enorm, spread, four):
    text_body(t_a, t_b, t_c, t_d, four)
    at = pl.multiple_of(rank[0] * ROWS, ROWS)
    embed = images[pl.ds(at, ROWS), :].astype(F32)
    embed = embed + jnp.sum(got[...].astype(F32), axis=0)
    norm = jnp.sqrt(jnp.sum(embed * embed, axis=-1, keepdims=True) + 1e-06)
    value = embed / norm
    unit[...] = value
    enorm[...] = jnp.broadcast_to(norm, (ROWS, 128))
    value = value.astype(BF)
    for k in range(NT):
        spread[k] = value


def pairs_body(rank, log_scale, bias, unit, *refs):
    du, c_own, c_oth, again = refs[8:]
    again[...] = unit[...]
    scale = jnp.exp(jnp.full((1, 1), log_scale[0], F32))
    u = unit[...].reshape(IMG, D)
    total = None
    for half, out in ((0, c_own), (4, c_oth)):
        texts = jnp.concatenate([ref[...].reshape(64, D) for ref in refs[half : half + 4]], axis=0)
        coef = jax.nn.sigmoid(scale * dot(u, texts, 1, 1) + bias[0])
        if half == 0:
            row = lax.broadcasted_iota(I32, (IMG, 256), 0) - rank[0] * ROWS
            col = lax.broadcasted_iota(I32, (IMG, 256), 1)
            coef = coef - jnp.where((row == col) & (col < ROWS), 1.0, 0.0)
        coef = coef.astype(BF)
        out[...] = coef
        part = dot(coef, texts)
        total = part if half == 0 else total + part
    du[...] = (scale * total).astype(BF).reshape(NT, ROWS, D)


def text_grad_body(log_scale, c_mine, u_mine, c_got, u_got, keep, *sent):
    scale = jnp.exp(jnp.full((1, 1), log_scale[0], F32))
    dw = dot(c_mine[...], u_mine[...].reshape(IMG, D), 0, 0)
    dw = scale * (dw + dot(c_got[...], u_got[...].reshape(IMG, D), 0, 0))
    keep[...] = dw[:64]
    for k in range(3):
        sent[k][...] = dw[64 * (k + 1) : 64 * (k + 2)].astype(BF)


def text_fold_body(keep, a, b, c, rest, *sent):
    dw = keep[...] + a[...].astype(F32) + b[...].astype(F32) + c[...].astype(F32)
    rest[...] = dw[:ROWS]
    for k in range(3):
        sent[k][...] = dw[ROWS * (k + 1) : ROWS * (k + 2)].astype(BF)


def embed_grad_body(got, unit, enorm, rows, spread):
    du = jnp.sum(got[...].astype(F32), axis=0)
    u = unit[...]
    de = (du - u * jnp.sum(u * du, axis=-1, keepdims=True)) / enorm[:, :1]
    de = de.astype(BF)
    rows[...] = de
    for k in range(NT):
        spread[k] = de


def slope_body(rank, de, w_out, slope, dpre, *sent):
    value = dot(de[...].reshape(IMG, D), w_out[...], 1, 1) * slope[...]
    dpre[...] = value.astype(BF)
    pack_body(rank, de, dpre, *sent)


def dn_body(dpre, w_in, keep, t_a, t_b, t_c, dn, rest, *sent):
    dn[...] = dot(dpre[...], w_in[...]).astype(BF).reshape(NT, ROWS, D)
    text_fold_body(keep, t_a, t_b, t_c, rest, *sent)


def pack(rank, left, right, lefts, rights):
    r = lax.broadcasted_iota(I32, (SEL, 1), 0)
    block = (r * 52429) >> 21
    place = r - block * 40
    base = jnp.where(place < COLS, block * 72 + place, -4096)
    diff = lax.broadcasted_iota(I32, (SEL, LANES), 1) - base
    for ref, at, x_flip, c_flip in lefts:
        x, c = rank[2] ^ x_flip, rank[1] ^ c_flip
        window = pl.ds(pl.multiple_of(x * 512, 512), LANES)
        one = jnp.where(diff == x * 64 + c * COLS, 1.0, 0.0).astype(BF)
        ref[at : at + SEL] = dot(one, left[:, :, window].reshape(IMG, LANES), 1, 1).astype(BF)
    wide = jnp.concatenate([right[...].astype(F32), jnp.zeros((IMG, LANES - FF_T), F32)], axis=1)
    wide = wide.astype(BF)
    for k in range(5):
        for ref, at in rights:
            ref[at + k * 128 : at + (k + 1) * 128] = wide[:, k * 128 : (k + 1) * 128]


def pack_relay_body(rank, left, right, mine, to_core, to_x):
    lefts = ((mine, 0, 0, 0), (to_core, 0, 0, 1), (to_x, 0, 1, 0), (to_x, SEL, 1, 1))
    pack(rank, left, right, lefts, ((to_core, SEL), (to_x, 2 * SEL)))


def pack_body(rank, left, right, mine, to_core, to_x, to_both):
    lefts = ((to_x, 0, 1, 0), (to_both, 0, 1, 1), (mine, 0, 0, 0), (to_core, 0, 0, 1))
    pack(rank, left, right, lefts, ((to_core, SEL), (to_x, SEL), (to_both, SEL)))


def weights_body(*refs):
    n_mine, n_own, n_core, n_x, n_xc = refs[:5]
    e_mine, e_own, e_core, e_x, e_xc = refs[5:10]
    out = refs[10]

    def left(*parts):
        return jnp.concatenate([ref[at : at + SEL] for ref, at in parts], axis=1)

    def right(*parts):
        rows = []
        for ref, at in parts:
            chunks = [ref[at + k * 128 : at + (k + 1) * 128] for k in range(5)]
            rows.append(jnp.concatenate(chunks, axis=1))
        return jnp.concatenate(rows, axis=0)

    in_part = dot(
        left((n_mine, 0), (n_core, 0), (n_x, 0), (n_xc, SEL)),
        right((e_own, SEL), (e_core, SEL), (e_x, SEL), (e_xc, SEL)),
    )
    out_part = dot(
        left((e_mine, 0), (e_core, 0), (e_x, 0), (e_xc, 0)),
        right((n_own, SEL), (n_core, SEL), (n_x, 2 * SEL), (n_xc, 2 * SEL)),
    )
    both = jnp.concatenate([in_part[:, :OUT_AT], out_part[:, :OUT_AT]], axis=1)
    for k in range(8):
        out[k] = both[k * 40 : (k + 1) * 40].astype(BF)


def image_body(rank, got, images, gain, de_rows, rows):
    dn = jnp.sum(got[...].astype(F32), axis=0)
    at = pl.multiple_of(rank[0] * ROWS, ROWS)
    xhat, sd = layer_stats(images[pl.ds(at, ROWS), :].astype(F32))
    dxh = dn * gain[...].reshape(1, D)
    grad = (
        dxh
        - jnp.mean(dxh, axis=-1, keepdims=True)
        - xhat * jnp.mean(dxh * xhat, axis=-1, keepdims=True)
    ) / sd
    rows[...] = (de_rows[...].astype(F32) + grad).astype(BF)


def place_body(rank, *refs):
    out = refs[NT]
    for ref, k in zip(refs[:NT], (0, 1, 2, 4, 6, 3, 5, 7)):
        at = pl.multiple_of((rank[0] ^ k) * ROWS, ROWS)
        out[pl.ds(at, ROWS), :] = ref[...].astype(F32)


def final_body(got, texts, rest, a, b, c, text_grad, in_grad, out_grad):
    total = got[0].astype(F32)
    for k in range(1, 8):
        total = total + got[k].astype(F32)
    in_grad[...] = total[:COLS, 0:FF_T]
    out_grad[...] = total[:COLS, OUT_AT : OUT_AT + FF_T]
    dw = rest[...] + a[...].astype(F32) + b[...].astype(F32) + c[...].astype(F32)
    tunit, tnorm = text_unit(texts[...].astype(F32))
    text_grad[...] = (dw - tunit * jnp.sum(tunit * dw, axis=-1, keepdims=True)) / tnorm


def local(images, gain, w_in, b_in, w_out, texts, log_scale, bias):
    rank_d = lax.axis_index("dp")
    rank_t = lax.axis_index("tensor")
    rank = jnp.stack([rank_t, rank_d % 2, rank_d // 16]).astype(I32)
    w_in = w_in.T
    block = sds((ROWS, D), BF)
    blocks = sds((NT, ROWS, D), BF)
    groups = [[x * 16 + k * 2 + c for k in range(8)] for x in range(2) for c in range(2)]

    def tensor_all(x):
        return lax.all_to_all(x, "tensor", 0, 0, tiled=True)

    def dp(x, mask):
        return swap(x, "dp", 32, mask)

    normed, hidden, slope, part = forward(images, gain, w_in, b_in, w_out)
    n_mine, n_own, n_tox = call(
        pack_relay_body,
        (sds((SEL, 128), BF), sds((3 * SEL, 128), BF), sds((4 * SEL, 128), BF)),
        (rank, hold(normed.reshape(NT, ROWS, D)), hold(hidden)),
        smem=(0,),
        hbm=(0, 1, 2),
        after=(part,),
        flops=2 * 100_000_000,
        size=2 << 20,
    )
    unit, enorm, spread, four = call(
        embed_body,
        (sds((ROWS, D), F32), sds((ROWS, 128), F32), blocks, sds((4, ROWS, D), BF)),
        (rank, images, tensor_all(part), texts, dp(texts, 4), dp(texts, 8), dp(texts, 12)),
        smem=(0,),
        hbm=(0, 1, 2, 3),
        after=(n_own,),
    )
    t_own = [four, dp(four, 2), dp(four, 16), dp(four, 18)]
    t_oth = [dp(x, 1) for x in t_own]
    unit_b = tensor_all(spread)
    du, c_own, c_oth, again = call(
        pairs_body,
        (blocks, sds((IMG, 256), BF), sds((IMG, 256), BF), blocks),
        (rank, log_scale, bias, unit_b, hold(four), *t_own[1:], *t_oth),
        smem=(0, 1, 2),
        hbm=(0, 1, 2, 3),
        flops=2 * 150_000_000,
        size=2 << 20,
    )
    u_got = dp(again, 1)
    c_got = dp(c_oth, 1)
    sixty = sds((4 * ROWS, D), BF)
    keep, *sent = call(
        text_grad_body,
        (sds((4 * ROWS, D), F32), sixty, sixty, sixty),
        (log_scale, hold(c_own), unit_b, c_got, u_got),
        smem=(0,),
        hbm=(0, 1, 2, 3),
        flops=2 * 75_000_000,
        size=2 << 20,
    )
    got = [dp(x, mask) for x, mask in zip(sent, (2, 16, 18))]
    n_core = dp(n_own, 1)
    n_x = dp(n_tox, 16)
    n_xc = dp(n_x, 1)
    de_rows, spread = call(
        embed_grad_body,
        (block, blocks),
        (tensor_all(du), hold(unit), hold(enorm)),
        hbm=(0, 1),
        after=(keep,),
    )
    de = tensor_all(spread)

    operand = sds((3 * SEL, 128), BF)
    dpre, e_mine, e_own, e_tox, e_toxc = call(
        slope_body,
        (sds((IMG, FF_T), BF), sds((SEL, 128), BF), operand, operand, operand),
        (rank, de, hold(w_out), hold(slope)),
        smem=(0,),
        hbm=(1, 2, 3, 4),
        after=(n_x,),
        flops=2 * 180_000_000,
        size=4 << 20,
    )
    e_x = dp(e_tox, 16)
    e_xc = dp(e_toxc, 17)
    e_core = dp(e_own, 1)
    dn, rest, *sent = call(
        dn_body,
        (blocks, sds((ROWS, D), F32), block, block, block),
        (dpre, w_in, hold(keep), *got),
        hbm=(0, 1, 2, 3, 4),
        after=(n_core, n_xc),
        flops=2 * 80_000_000,
        size=2 << 20,
    )
    dn = tensor_all(dn)
    got = [dp(x, mask) for x, mask in zip(sent, (4, 8, 12))]
    rows = call(
        image_body, block, (rank, dn, images, gain, de_rows), smem=(0,), hbm=(0,)
    )
    payload = call(
        weights_body,
        sds((8, 40, D), BF),
        (hold(n_mine), hold(n_own), n_core, n_x, n_xc)
        + (hold(e_mine), hold(e_own), e_core, e_x, e_xc),
        hbm=(0,),
        after=(rows, *got),
        flops=2 * 160_000_000,
        size=3 << 20,
    )
    total = lax.all_to_all(payload, "dp", 0, 0, tiled=True, axis_index_groups=groups)

    spread = [rows] + [swap(rows, "tensor", NT, k) for k in (1, 2, 4, 6)]
    spread += [swap(spread[1], "tensor", NT, k) for k in (2, 4, 6)]
    image_grad = call(place_body, sds((IMG, D), F32), (rank, *spread), smem=(0,))
    text_grad, in_grad, out_grad = call(
        final_body,
        (sds((ROWS, D), F32), sds((COLS, FF_T), F32), sds((COLS, FF_T), F32)),
        (total, texts, rest, *got),
    )
    return (image_grad, text_grad, in_grad, out_grad)


def solution(mesh):
    return jax.shard_map(
        local,
        mesh=mesh,
        in_specs=(
            P("dp", None),
            P(),
            P(None, "tensor"),
            P("tensor"),
            P("tensor", None),
            P(("dp", "tensor"), None),
            P(),
            P(),
        ),
        out_specs=(P("dp", None), P(("dp", "tensor"), None), P("dp", "tensor"), P("dp", "tensor")),
        check_vma=False,
    )
```

```python
import jax
import jax.numpy as jnp
from jax import lax
from jax.experimental import pallas as pl
from jax.experimental.pallas import tpu as pltpu
from jax.sharding import PartitionSpec as P

F32 = jnp.float32
BF = jnp.bfloat16
I32 = jnp.int32
D = 1152
FF_T = 538
NT = 8
ROWS = 16
COLS = 36
IMG = 128
SEL = 320
LANES = 640
OUT_AT = 576
ROOT = 0.7978845608028654


def dot(a, b, ca=1, cb=0):
    return lax.dot_general(a, b, (((ca,), (cb,)), ((), ())), preferred_element_type=F32)


def swap(x, axis, n, mask):
    return lax.ppermute(x, axis, [(i, i ^ mask) for i in range(n)])


def sds(shape, dtype):
    return jax.ShapeDtypeStruct(shape, dtype)


def hold(x):
    return pltpu.with_memory_space_constraint(x, pltpu.HBM)


def call(body, outs, args, scratch=(), smem=(), after=(), beside=(), hbm=(), flops=0, size=1 << 20):
    single = not isinstance(outs, (tuple, list))
    outs = (outs,) if single else tuple(outs)
    vm = pl.BlockSpec(memory_space=pltpu.VMEM)
    sm = pl.BlockSpec(memory_space=pltpu.SMEM)
    some = pl.BlockSpec(memory_space=pl.ANY)
    far = pl.BlockSpec(memory_space=pltpu.HBM)
    order = [hold(x) for x in after] + list(beside)
    n_in, n_after, n_out, n_far = len(args), len(order), len(outs), len(hbm)

    def kernel(*refs):
        ins = refs[:n_in]
        results = list(refs[n_in + n_after : n_in + n_after + n_out])
        rest = refs[n_in + n_after + n_out :]
        near, sems, own = rest[:n_far], rest[n_far : 2 * n_far], rest[2 * n_far :]
        copies = []
        for ref, at, sem in zip(near, hbm, sems):
            copies.append(pltpu.make_async_copy(ref, results[at], sem))
            results[at] = ref
        body(*ins, *results, *own)
        for copy in copies:
            copy.start()
        for copy in copies:
            copy.wait()

    got = pl.pallas_call(
        kernel,
        out_shape=tuple(
            pltpu.HBM(o.shape, o.dtype) if i in hbm else o for i, o in enumerate(outs)
        ),
        in_specs=[sm if i in smem else vm for i in range(n_in)] + [some] * n_after,
        out_specs=tuple(far if i in hbm else vm for i in range(n_out)),
        scratch_shapes=[pltpu.VMEM(outs[i].shape, outs[i].dtype) for i in hbm]
        + [pltpu.SemaphoreType.DMA(()) for _ in hbm]
        + list(scratch),
        compiler_params=pltpu.CompilerParams(vmem_limit_bytes=24 << 20),
        cost_estimate=pl.CostEstimate(flops=flops, bytes_accessed=size, transcendentals=0),
    )(*args, *order)
    return got[0] if single else got


def text_unit(tf):
    tnorm = jnp.sqrt(jnp.sum(tf * tf, axis=-1, keepdims=True) + 1e-06)
    return tf / tnorm, tnorm


def text_body(mine, *refs):
    out = refs[3]
    for k, ref in enumerate((mine,) + refs[:3]):
        out[k] = text_unit(ref[...].astype(F32))[0].astype(BF)


def layer_stats(xf):
    centered = xf - jnp.mean(xf, axis=-1, keepdims=True)
    sd = jnp.sqrt(jnp.mean(centered * centered, axis=-1, keepdims=True) + 1e-06)
    return centered / sd, sd


def forward_body(images, gain, w_in, b_in, w_out, normed, hidden, slope, part, *scratch):
    v_images, v_in, v_out, v_normed, v_hidden, v_slope, v_part, sem = scratch

    def move(src, dst, k):
        copy = pltpu.make_async_copy(src, dst, sem.at[k])
        copy.start()
        return copy

    get_images = move(images, v_images, 0)
    get_in = move(w_in, v_in, 1)
    get_out = move(w_out, v_out, 2)
    get_images.wait()
    xhat, _ = layer_stats(v_images[...].astype(F32))
    normed_b = (xhat * gain[...].reshape(1, D)).astype(BF)
    v_normed[...] = normed_b
    put_normed = move(v_normed, normed, 3)
    get_in.wait()
    pre = dot(normed_b, v_in[...], 1, 1) + b_in[...].reshape(1, FF_T)
    square = pre * pre
    th = jnp.tanh(ROOT * (pre + 0.044715 * (square * pre)))
    cdf = 0.5 * (1.0 + th)
    hidden_b = (pre * cdf).astype(BF)
    v_hidden[...] = hidden_b
    put_hidden = move(v_hidden, hidden, 4)
    v_slope[...] = cdf + 0.5 * pre * (1.0 - th * th) * (ROOT * (1.0 + 0.134145 * square))
    put_slope = move(v_slope, slope, 6)
    get_out.wait()
    v_part[...] = dot(hidden_b, v_out[...]).astype(BF).reshape(NT, ROWS, D)
    put_part = move(v_part, part, 5)
    for copy in (put_normed, put_hidden, put_part, put_slope):
        copy.wait()


def forward(images, gain, w_in, b_in, w_out):
    far = pl.BlockSpec(memory_space=pltpu.HBM)
    near = pl.BlockSpec(memory_space=pltpu.VMEM)

    shapes = (
        ((IMG, D), BF),
        ((IMG, FF_T), BF),
        ((IMG, FF_T), F32),
        ((NT, ROWS, D), BF),
    )
    return pl.pallas_call(
        forward_body,
        out_shape=tuple(pltpu.HBM(*shape) for shape in shapes),
        in_specs=[far, near, far, near, far],
        out_specs=(far,) * 4,
        scratch_shapes=[
            pltpu.VMEM((IMG, D), BF),
            pltpu.VMEM((FF_T, D), BF),
            pltpu.VMEM((FF_T, D), BF),
        ]
        + [pltpu.VMEM(*shape) for shape in shapes]
        + [pltpu.SemaphoreType.DMA((7,))],
        compiler_params=pltpu.CompilerParams(vmem_limit_bytes=24 << 20),
        cost_estimate=pl.CostEstimate(
            flops=2 * 160_000_000, bytes_accessed=4 << 20, transcendentals=0
        ),
    )(hold(images), hold(gain), hold(w_in), hold(b_in), hold(w_out))


def embed_body(rank, images, got, t_a, t_b, t_c, t_d, unit, enorm, spread, four):
    text_body(t_a, t_b, t_c, t_d, four)
    at = pl.multiple_of(rank[0] * ROWS, ROWS)
    embed = images[pl.ds(at, ROWS), :].astype(F32)
    embed = embed + jnp.sum(got[...].astype(F32), axis=0)
    norm = jnp.sqrt(jnp.sum(embed * embed, axis=-1, keepdims=True) + 1e-06)
    value = embed / norm
    unit[...] = value
    enorm[...] = jnp.broadcast_to(norm, (ROWS, 128))
    value = value.astype(BF)
    for k in range(NT):
        spread[k] = value


def pairs_body(rank, log_scale, bias, unit, *refs):
    du, c_own, c_oth, again = refs[8:]
    again[...] = unit[...]
    scale = jnp.exp(jnp.full((1, 1), log_scale[0], F32))
    u = unit[...].reshape(IMG, D)
    total = None
    for half, out in ((0, c_own), (4, c_oth)):
        texts = jnp.concatenate([ref[...].reshape(64, D) for ref in refs[half : half + 4]], axis=0)
        coef = jax.nn.sigmoid(scale * dot(u, texts, 1, 1) + bias[0])
        if half == 0:
            row = lax.broadcasted_iota(I32, (IMG, 256), 0) - rank[0] * ROWS
            col = lax.broadcasted_iota(I32, (IMG, 256), 1)
            coef = coef - jnp.where((row == col) & (col < ROWS), 1.0, 0.0)
        coef = coef.astype(BF)
        out[...] = coef
        part = dot(coef, texts)
        total = part if half == 0 else total + part
    du[...] = (scale * total).astype(BF).reshape(NT, ROWS, D)


def text_grad_body(log_scale, c_mine, u_mine, c_got, u_got, keep, *sent):
    scale = jnp.exp(jnp.full((1, 1), log_scale[0], F32))
    dw = dot(c_mine[...], u_mine[...].reshape(IMG, D), 0, 0)
    dw = scale * (dw + dot(c_got[...], u_got[...].reshape(IMG, D), 0, 0))
    keep[...] = dw[:64]
    for k in range(3):
        sent[k][...] = dw[64 * (k + 1) : 64 * (k + 2)].astype(BF)


def text_fold_body(keep, a, b, c, rest, *sent):
    dw = keep[...] + a[...].astype(F32) + b[...].astype(F32) + c[...].astype(F32)
    rest[...] = dw[:ROWS]
    for k in range(3):
        sent[k][...] = dw[ROWS * (k + 1) : ROWS * (k + 2)].astype(BF)


def embed_grad_body(got, unit, enorm, rows, spread):
    du = jnp.sum(got[...].astype(F32), axis=0)
    u = unit[...]
    de = (du - u * jnp.sum(u * du, axis=-1, keepdims=True)) / enorm[:, :1]
    de = de.astype(BF)
    rows[...] = de
    for k in range(NT):
        spread[k] = de


def slope_body(rank, de, w_out, slope, dpre, *sent):
    value = dot(de[...].reshape(IMG, D), w_out[...], 1, 1) * slope[...]
    dpre[...] = value.astype(BF)
    pack_body(rank, de, dpre, *sent)


def dn_body(dpre, w_in, keep, t_a, t_b, t_c, dn, rest, *sent):
    dn[...] = dot(dpre[...], w_in[...]).astype(BF).reshape(NT, ROWS, D)
    text_fold_body(keep, t_a, t_b, t_c, rest, *sent)


def pack(rank, left, right, lefts, rights):
    r = lax.broadcasted_iota(I32, (SEL, 1), 0)
    block = (r * 52429) >> 21
    place = r - block * 40
    base = jnp.where(place < COLS, block * 72 + place, -4096)
    diff = lax.broadcasted_iota(I32, (SEL, LANES), 1) - base
    for ref, at, x_flip, c_flip in lefts:
        x, c = rank[2] ^ x_flip, rank[1] ^ c_flip
        window = pl.ds(pl.multiple_of(x * 512, 512), LANES)
        one = jnp.where(diff == x * 64 + c * COLS, 1.0, 0.0).astype(BF)
        ref[at : at + SEL] = dot(one, left[:, :, window].reshape(IMG, LANES), 1, 1).astype(BF)
    wide = jnp.concatenate([right[...].astype(F32), jnp.zeros((IMG, LANES - FF_T), F32)], axis=1)
    wide = wide.astype(BF)
    for k in range(5):
        for ref, at in rights:
            ref[at + k * 128 : at + (k + 1) * 128] = wide[:, k * 128 : (k + 1) * 128]


def pack_relay_body(rank, left, right, mine, to_core, to_x):
    lefts = ((mine, 0, 0, 0), (to_core, 0, 0, 1), (to_x, 0, 1, 0), (to_x, SEL, 1, 1))
    pack(rank, left, right, lefts, ((to_core, SEL), (to_x, 2 * SEL)))


def pack_body(rank, left, right, mine, to_core, to_x, to_both):
    lefts = ((to_x, 0, 1, 0), (to_both, 0, 1, 1), (mine, 0, 0, 0), (to_core, 0, 0, 1))
    pack(rank, left, right, lefts, ((to_core, SEL), (to_x, SEL), (to_both, SEL)))


def weights_body(*refs):
    n_mine, n_own, n_core, n_x, n_xc = refs[:5]
    e_mine, e_own, e_core, e_x, e_xc = refs[5:10]
    out = refs[10]

    def left(*parts):
        return jnp.concatenate([ref[at : at + SEL] for ref, at in parts], axis=1)

    def right(*parts):
        rows = []
        for ref, at in parts:
            chunks = [ref[at + k * 128 : at + (k + 1) * 128] for k in range(5)]
            rows.append(jnp.concatenate(chunks, axis=1))
        return jnp.concatenate(rows, axis=0)

    in_part = dot(
        left((n_mine, 0), (n_core, 0), (n_x, 0), (n_xc, SEL)),
        right((e_own, SEL), (e_core, SEL), (e_x, SEL), (e_xc, SEL)),
    )
    out_part = dot(
        left((e_mine, 0), (e_core, 0), (e_x, 0), (e_xc, 0)),
        right((n_own, SEL), (n_core, SEL), (n_x, 2 * SEL), (n_xc, 2 * SEL)),
    )
    both = jnp.concatenate([in_part[:, :OUT_AT], out_part[:, :OUT_AT]], axis=1)
    for k in range(8):
        out[k] = both[k * 40 : (k + 1) * 40].astype(BF)


def image_body(rank, got, images, gain, de_rows, rows):
    dn = jnp.sum(got[...].astype(F32), axis=0)
    at = pl.multiple_of(rank[0] * ROWS, ROWS)
    xhat, sd = layer_stats(images[pl.ds(at, ROWS), :].astype(F32))
    dxh = dn * gain[...].reshape(1, D)
    grad = (
        dxh
        - jnp.mean(dxh, axis=-1, keepdims=True)
        - xhat * jnp.mean(dxh * xhat, axis=-1, keepdims=True)
    ) / sd
    rows[...] = (de_rows[...].astype(F32) + grad).astype(BF)


def place_body(rank, *refs):
    out = refs[NT]
    for ref, k in zip(refs[:NT], (0, 1, 2, 4, 6, 3, 5, 7)):
        at = pl.multiple_of((rank[0] ^ k) * ROWS, ROWS)
        out[pl.ds(at, ROWS), :] = ref[...].astype(F32)


def final_body(got, texts, rest, a, b, c, text_grad, in_grad, out_grad):
    total = got[0].astype(F32)
    for k in range(1, 8):
        total = total + got[k].astype(F32)
    in_grad[...] = total[:COLS, 0:FF_T]
    out_grad[...] = total[:COLS, OUT_AT : OUT_AT + FF_T]
    dw = rest[...] + a[...].astype(F32) + b[...].astype(F32) + c[...].astype(F32)
    tunit, tnorm = text_unit(texts[...].astype(F32))
    text_grad[...] = (dw - tunit * jnp.sum(tunit * dw, axis=-1, keepdims=True)) / tnorm


def local(images, gain, w_in, b_in, w_out, texts, log_scale, bias):
    rank_d = lax.axis_index("dp")
    rank_t = lax.axis_index("tensor")
    rank = jnp.stack([rank_t, rank_d % 2, rank_d // 16]).astype(I32)
    w_in = w_in.T
    block = sds((ROWS, D), BF)
    blocks = sds((NT, ROWS, D), BF)
    groups = [[x * 16 + k * 2 + c for k in range(8)] for x in range(2) for c in range(2)]

    def tensor_all(x):
        return lax.all_to_all(x, "tensor", 0, 0, tiled=True)

    def dp(x, mask):
        return swap(x, "dp", 32, mask)

    normed, hidden, slope, part = forward(images, gain, w_in, b_in, w_out)
    n_mine, n_own, n_tox = call(
        pack_relay_body,
        (sds((SEL, 128), BF), sds((3 * SEL, 128), BF), sds((4 * SEL, 128), BF)),
        (rank, hold(normed.reshape(NT, ROWS, D)), hold(hidden)),
        smem=(0,),
        hbm=(0, 1, 2),
        after=(part,),
        flops=2 * 100_000_000,
        size=2 << 20,
    )
    unit, enorm, spread, four = call(
        embed_body,
        (sds((ROWS, D), F32), sds((ROWS, 128), F32), blocks, sds((4, ROWS, D), BF)),
        (rank, images, tensor_all(part), texts, dp(texts, 4), dp(texts, 8), dp(texts, 12)),
        smem=(0,),
        hbm=(0, 1, 2, 3),
        after=(n_own,),
    )
    t_own = [four, dp(four, 2), dp(four, 16), dp(four, 18)]
    t_oth = [dp(x, 1) for x in t_own]
    unit_b = tensor_all(spread)
    du, c_own, c_oth, again = call(
        pairs_body,
        (blocks, sds((IMG, 256), BF), sds((IMG, 256), BF), blocks),
        (rank, log_scale, bias, unit_b, hold(four), *t_own[1:], *t_oth),
        smem=(0, 1, 2),
        hbm=(0, 1, 2, 3),
        flops=2 * 150_000_000,
        size=2 << 20,
    )
    u_got = dp(again, 1)
    c_got = dp(c_oth, 1)
    sixty = sds((4 * ROWS, D), BF)
    keep, *sent = call(
        text_grad_body,
        (sds((4 * ROWS, D), F32), sixty, sixty, sixty),
        (log_scale, hold(c_own), unit_b, c_got, u_got),
        smem=(0,),
        hbm=(0, 1, 2, 3),
        flops=2 * 75_000_000,
        size=2 << 20,
    )
    got = [dp(x, mask) for x, mask in zip(sent, (2, 16, 18))]
    n_core = dp(n_own, 1)
    n_x = dp(n_tox, 16)
    n_xc = dp(n_x, 1)
    de_rows, spread = call(
        embed_grad_body,
        (block, blocks),
        (tensor_all(du), unit, enorm),
        hbm=(0, 1),
        after=(keep,),
    )
    de = tensor_all(spread)

    operand = sds((3 * SEL, 128), BF)
    dpre, e_mine, e_own, e_tox, e_toxc = call(
        slope_body,
        (sds((IMG, FF_T), BF), sds((SEL, 128), BF), operand, operand, operand),
        (rank, de, hold(w_out), hold(slope)),
        smem=(0,),
        hbm=(1, 2, 3, 4),
        beside=(n_x,),
        flops=2 * 180_000_000,
        size=4 << 20,
    )
    e_x = dp(e_tox, 16)
    e_xc = dp(e_toxc, 17)
    e_core = dp(e_own, 1)
    dn, rest, *sent = call(
        dn_body,
        (blocks, sds((ROWS, D), F32), block, block, block),
        (dpre, w_in, keep, *got),
        hbm=(0, 1, 2, 3, 4),
        beside=(n_core, n_xc),
        flops=2 * 80_000_000,
        size=2 << 20,
    )
    dn = tensor_all(dn)
    got = [dp(x, mask) for x, mask in zip(sent, (4, 8, 12))]
    rows = call(
        image_body, block, (rank, dn, images, gain, de_rows), smem=(0,), hbm=(0,)
    )
    payload = call(
        weights_body,
        sds((8, 40, D), BF),
        (n_mine, n_own, n_core, n_x, n_xc)
        + (hold(e_mine), hold(e_own), e_core, e_x, e_xc),
        hbm=(0,),
        after=(rows,),
        beside=got,
        flops=2 * 160_000_000,
        size=3 << 20,
    )
    total = lax.all_to_all(payload, "dp", 0, 0, tiled=True, axis_index_groups=groups)

    spread = [rows] + [swap(rows, "tensor", NT, k) for k in (1, 2, 4, 6)]
    spread += [swap(spread[1], "tensor", NT, k) for k in (2, 4, 6)]
    image_grad = call(place_body, sds((IMG, D), F32), (rank, *spread), smem=(0,))
    text_grad, in_grad, out_grad = call(
        final_body,
        (sds((ROWS, D), F32), sds((COLS, FF_T), F32), sds((COLS, FF_T), F32)),
        (total, texts, rest, *got),
    )
    return (image_grad, text_grad, in_grad, out_grad)


def solution(mesh):
    return jax.shard_map(
        local,
        mesh=mesh,
        in_specs=(
            P("dp", None),
            P(),
            P(None, "tensor"),
            P("tensor"),
            P("tensor", None),
            P(("dp", "tensor"), None),
            P(),
            P(),
        ),
        out_specs=(P("dp", None), P(("dp", "tensor"), None), P("dp", "tensor"), P("dp", "tensor")),
        check_vma=False,
    )
```

```python
import jax
import jax.numpy as jnp
from jax import lax
from jax.experimental import pallas as pl
from jax.experimental.pallas import tpu as pltpu
from jax.sharding import PartitionSpec as P

F32 = jnp.float32
BF = jnp.bfloat16
I32 = jnp.int32
D = 1152
FF_T = 538
NT = 8
ROWS = 16
COLS = 36
IMG = 128
SEL = 320
LANES = 640
OUT_AT = 576
ROOT = 0.7978845608028654


def dot(a, b, ca=1, cb=0):
    return lax.dot_general(a, b, (((ca,), (cb,)), ((), ())), preferred_element_type=F32)


def swap(x, axis, n, mask):
    return lax.ppermute(x, axis, [(i, i ^ mask) for i in range(n)])


def sds(shape, dtype):
    return jax.ShapeDtypeStruct(shape, dtype)


def hold(x):
    return pltpu.with_memory_space_constraint(x, pltpu.HBM)


def call(body, outs, args, scratch=(), smem=(), after=(), beside=(), hbm=(), flops=0, size=1 << 20):
    single = not isinstance(outs, (tuple, list))
    outs = (outs,) if single else tuple(outs)
    vm = pl.BlockSpec(memory_space=pltpu.VMEM)
    sm = pl.BlockSpec(memory_space=pltpu.SMEM)
    some = pl.BlockSpec(memory_space=pl.ANY)
    far = pl.BlockSpec(memory_space=pltpu.HBM)
    order = [hold(x) for x in after] + list(beside)
    n_in, n_after, n_out, n_far = len(args), len(order), len(outs), len(hbm)

    def kernel(*refs):
        ins = refs[:n_in]
        results = list(refs[n_in + n_after : n_in + n_after + n_out])
        rest = refs[n_in + n_after + n_out :]
        near, sems, own = rest[:n_far], rest[n_far : 2 * n_far], rest[2 * n_far :]
        copies = []
        for ref, at, sem in zip(near, hbm, sems):
            copies.append(pltpu.make_async_copy(ref, results[at], sem))
            results[at] = ref
        body(*ins, *results, *own)
        for copy in copies:
            copy.start()
        for copy in copies:
            copy.wait()

    got = pl.pallas_call(
        kernel,
        out_shape=tuple(
            pltpu.HBM(o.shape, o.dtype) if i in hbm else o for i, o in enumerate(outs)
        ),
        in_specs=[sm if i in smem else vm for i in range(n_in)] + [some] * n_after,
        out_specs=tuple(far if i in hbm else vm for i in range(n_out)),
        scratch_shapes=[pltpu.VMEM(outs[i].shape, outs[i].dtype) for i in hbm]
        + [pltpu.SemaphoreType.DMA(()) for _ in hbm]
        + list(scratch),
        compiler_params=pltpu.CompilerParams(vmem_limit_bytes=24 << 20),
        cost_estimate=pl.CostEstimate(flops=flops, bytes_accessed=size, transcendentals=0),
    )(*args, *order)
    return got[0] if single else got


def text_unit(tf):
    tnorm = jnp.sqrt(jnp.sum(tf * tf, axis=-1, keepdims=True) + 1e-06)
    return tf / tnorm, tnorm


def text_body(mine, *refs):
    out = refs[3]
    for k, ref in enumerate((mine,) + refs[:3]):
        out[k] = text_unit(ref[...].astype(F32))[0].astype(BF)


def layer_stats(xf):
    centered = xf - jnp.mean(xf, axis=-1, keepdims=True)
    sd = jnp.sqrt(jnp.mean(centered * centered, axis=-1, keepdims=True) + 1e-06)
    return centered / sd, sd


def forward_body(images, gain, w_in, b_in, w_out, normed, hidden, slope, part, *scratch):
    v_images, v_in, v_out, v_normed, v_hidden, v_slope, v_part, sem = scratch

    def move(src, dst, k):
        copy = pltpu.make_async_copy(src, dst, sem.at[k])
        copy.start()
        return copy

    get_images = move(images, v_images, 0)
    get_in = move(w_in, v_in, 1)
    get_out = move(w_out, v_out, 2)
    get_images.wait()
    xhat, _ = layer_stats(v_images[...].astype(F32))
    normed_b = (xhat * gain[...].reshape(1, D)).astype(BF)
    v_normed[...] = normed_b
    put_normed = move(v_normed, normed, 3)
    get_in.wait()
    pre = dot(normed_b, v_in[...], 1, 1) + b_in[...].reshape(1, FF_T)
    square = pre * pre
    th = jnp.tanh(ROOT * (pre + 0.044715 * (square * pre)))
    cdf = 0.5 * (1.0 + th)
    hidden_b = (pre * cdf).astype(BF)
    v_hidden[...] = hidden_b
    put_hidden = move(v_hidden, hidden, 4)
    v_slope[...] = cdf + 0.5 * pre * (1.0 - th * th) * (ROOT * (1.0 + 0.134145 * square))
    put_slope = move(v_slope, slope, 6)
    get_out.wait()
    v_part[...] = dot(hidden_b, v_out[...]).astype(BF).reshape(NT, ROWS, D)
    put_part = move(v_part, part, 5)
    for copy in (put_normed, put_hidden, put_part, put_slope):
        copy.wait()


def forward(images, gain, w_in, b_in, w_out):
    far = pl.BlockSpec(memory_space=pltpu.HBM)
    near = pl.BlockSpec(memory_space=pltpu.VMEM)

    shapes = (
        ((IMG, D), BF),
        ((IMG, FF_T), BF),
        ((IMG, FF_T), F32),
        ((NT, ROWS, D), BF),
    )
    return pl.pallas_call(
        forward_body,
        out_shape=tuple(pltpu.HBM(*shape) for shape in shapes),
        in_specs=[far, near, far, near, far],
        out_specs=(far,) * 4,
        scratch_shapes=[
            pltpu.VMEM((IMG, D), BF),
            pltpu.VMEM((FF_T, D), BF),
            pltpu.VMEM((FF_T, D), BF),
        ]
        + [pltpu.VMEM(*shape) for shape in shapes]
        + [pltpu.SemaphoreType.DMA((7,))],
        compiler_params=pltpu.CompilerParams(vmem_limit_bytes=24 << 20),
        cost_estimate=pl.CostEstimate(
            flops=2 * 160_000_000, bytes_accessed=4 << 20, transcendentals=0
        ),
    )(hold(images), hold(gain), hold(w_in), hold(b_in), hold(w_out))


def embed_body(rank, images, got, t_a, t_b, t_c, t_d, unit, enorm, spread, four):
    text_body(t_a, t_b, t_c, t_d, four)
    at = pl.multiple_of(rank[0] * ROWS, ROWS)
    embed = images[pl.ds(at, ROWS), :].astype(F32)
    embed = embed + jnp.sum(got[...].astype(F32), axis=0)
    norm = jnp.sqrt(jnp.sum(embed * embed, axis=-1, keepdims=True) + 1e-06)
    value = embed / norm
    unit[...] = value
    enorm[...] = jnp.broadcast_to(norm, (ROWS, 128))
    value = value.astype(BF)
    for k in range(NT):
        spread[k] = value


def pairs_body(rank, log_scale, bias, unit, *refs):
    du, c_own, c_oth, again = refs[8:]
    again[...] = unit[...]
    scale = jnp.exp(jnp.full((1, 1), log_scale[0], F32))
    u = unit[...].reshape(IMG, D)
    total = None
    for half, out in ((0, c_own), (4, c_oth)):
        texts = jnp.concatenate([ref[...].reshape(64, D) for ref in refs[half : half + 4]], axis=0)
        coef = jax.nn.sigmoid(scale * dot(u, texts, 1, 1) + bias[0])
        if half == 0:
            row = lax.broadcasted_iota(I32, (IMG, 256), 0) - rank[0] * ROWS
            col = lax.broadcasted_iota(I32, (IMG, 256), 1)
            coef = coef - jnp.where((row == col) & (col < ROWS), 1.0, 0.0)
        coef = coef.astype(BF)
        out[...] = coef
        part = dot(coef, texts)
        total = part if half == 0 else total + part
    du[...] = (scale * total).astype(BF).reshape(NT, ROWS, D)


def text_grad_body(log_scale, c_mine, u_mine, c_got, u_got, keep, *sent):
    scale = jnp.exp(jnp.full((1, 1), log_scale[0], F32))
    dw = dot(c_mine[...], u_mine[...].reshape(IMG, D), 0, 0)
    dw = scale * (dw + dot(c_got[...], u_got[...].reshape(IMG, D), 0, 0))
    keep[...] = dw[:64]
    for k in range(3):
        sent[k][...] = dw[64 * (k + 1) : 64 * (k + 2)].astype(BF)


def text_fold_body(keep, a, b, c, rest, *sent):
    dw = keep[...] + a[...].astype(F32) + b[...].astype(F32) + c[...].astype(F32)
    rest[...] = dw[:ROWS]
    for k in range(3):
        sent[k][...] = dw[ROWS * (k + 1) : ROWS * (k + 2)].astype(BF)


def embed_grad_body(got, unit, enorm, rows, spread):
    du = jnp.sum(got[...].astype(F32), axis=0)
    u = unit[...]
    de = (du - u * jnp.sum(u * du, axis=-1, keepdims=True)) / enorm[:, :1]
    de = de.astype(BF)
    rows[...] = de
    for k in range(NT):
        spread[k] = de


def slope_body(rank, de, w_out, slope, dpre, *sent):
    value = dot(de[...].reshape(IMG, D), w_out[...], 1, 1) * slope[...]
    dpre[...] = value.astype(BF)
    pack_body(rank, de, dpre, *sent)


def dn_body(dpre, w_in, keep, t_a, t_b, t_c, dn, rest, *sent):
    dn[...] = dot(dpre[...], w_in[...]).astype(BF).reshape(NT, ROWS, D)
    text_fold_body(keep, t_a, t_b, t_c, rest, *sent)


def pack(rank, left, right, lefts, rights):
    r = lax.broadcasted_iota(I32, (SEL, 1), 0)
    block = (r * 52429) >> 21
    place = r - block * 40
    base = jnp.where(place < COLS, block * 72 + place, -4096)
    diff = lax.broadcasted_iota(I32, (SEL, LANES), 1) - base
    for ref, at, x_flip, c_flip in lefts:
        x, c = rank[2] ^ x_flip, rank[1] ^ c_flip
        window = pl.ds(pl.multiple_of(x * 512, 512), LANES)
        one = jnp.where(diff == x * 64 + c * COLS, 1.0, 0.0).astype(BF)
        ref[at : at + SEL] = dot(one, left[:, :, window].reshape(IMG, LANES), 1, 1).astype(BF)
    wide = jnp.concatenate([right[...].astype(F32), jnp.zeros((IMG, LANES - FF_T), F32)], axis=1)
    wide = wide.astype(BF)
    for k in range(5):
        for ref, at in rights:
            ref[at + k * 128 : at + (k + 1) * 128] = wide[:, k * 128 : (k + 1) * 128]


def pack_relay_body(rank, left, right, mine, to_core, to_x):
    lefts = ((mine, 0, 0, 0), (to_core, 0, 0, 1), (to_x, 0, 1, 0), (to_x, SEL, 1, 1))
    pack(rank, left, right, lefts, ((to_core, SEL), (to_x, 2 * SEL)))


def pack_body(rank, left, right, mine, to_core, to_x, to_both):
    lefts = ((to_x, 0, 1, 0), (to_both, 0, 1, 1), (mine, 0, 0, 0), (to_core, 0, 0, 1))
    pack(rank, left, right, lefts, ((to_core, SEL), (to_x, SEL), (to_both, SEL)))


def weights_body(*refs):
    n_mine, n_own, n_core, n_x, n_xc = refs[:5]
    e_mine, e_own, e_core, e_x, e_xc = refs[5:10]
    out = refs[10]

    def left(*parts):
        return jnp.concatenate([ref[at : at + SEL] for ref, at in parts], axis=1)

    def right(*parts):
        rows = []
        for ref, at in parts:
            chunks = [ref[at + k * 128 : at + (k + 1) * 128] for k in range(5)]
            rows.append(jnp.concatenate(chunks, axis=1))
        return jnp.concatenate(rows, axis=0)

    in_part = dot(
        left((n_mine, 0), (n_core, 0), (n_x, 0), (n_xc, SEL)),
        right((e_own, SEL), (e_core, SEL), (e_x, SEL), (e_xc, SEL)),
    )
    out_part = dot(
        left((e_mine, 0), (e_core, 0), (e_x, 0), (e_xc, 0)),
        right((n_own, SEL), (n_core, SEL), (n_x, 2 * SEL), (n_xc, 2 * SEL)),
    )
    both = jnp.concatenate([in_part[:, :OUT_AT], out_part[:, :OUT_AT]], axis=1)
    for k in range(8):
        out[k] = both[k * 40 : (k + 1) * 40].astype(BF)


def image_body(rank, got, images, gain, de_rows, rows):
    dn = jnp.sum(got[...].astype(F32), axis=0)
    at = pl.multiple_of(rank[0] * ROWS, ROWS)
    xhat, sd = layer_stats(images[pl.ds(at, ROWS), :].astype(F32))
    dxh = dn * gain[...].reshape(1, D)
    grad = (
        dxh
        - jnp.mean(dxh, axis=-1, keepdims=True)
        - xhat * jnp.mean(dxh * xhat, axis=-1, keepdims=True)
    ) / sd
    rows[...] = (de_rows[...].astype(F32) + grad).astype(BF)


def place_body(rank, *refs):
    out = refs[NT]
    for ref, k in zip(refs[:NT], (0, 1, 2, 4, 6, 3, 5, 7)):
        at = pl.multiple_of((rank[0] ^ k) * ROWS, ROWS)
        out[pl.ds(at, ROWS), :] = ref[...].astype(F32)


def final_body(got, texts, rest, a, b, c, text_grad, in_grad, out_grad):
    total = got[0].astype(F32)
    for k in range(1, 8):
        total = total + got[k].astype(F32)
    in_grad[...] = total[:COLS, 0:FF_T]
    out_grad[...] = total[:COLS, OUT_AT : OUT_AT + FF_T]
    dw = rest[...] + a[...].astype(F32) + b[...].astype(F32) + c[...].astype(F32)
    tunit, tnorm = text_unit(texts[...].astype(F32))
    text_grad[...] = (dw - tunit * jnp.sum(tunit * dw, axis=-1, keepdims=True)) / tnorm


def local(images, gain, w_in, b_in, w_out, texts, log_scale, bias):
    rank_d = lax.axis_index("dp")
    rank_t = lax.axis_index("tensor")
    rank = jnp.stack([rank_t, rank_d % 2, rank_d // 16]).astype(I32)
    w_in = w_in.T
    block = sds((ROWS, D), BF)
    blocks = sds((NT, ROWS, D), BF)
    groups = [[x * 16 + k * 2 + c for k in range(8)] for x in range(2) for c in range(2)]

    def tensor_all(x):
        return lax.all_to_all(x, "tensor", 0, 0, tiled=True)

    def dp(x, mask):
        return swap(x, "dp", 32, mask)

    normed, hidden, slope, part = forward(images, gain, w_in, b_in, w_out)
    n_mine, n_own, n_tox = call(
        pack_relay_body,
        (sds((SEL, 128), BF), sds((3 * SEL, 128), BF), sds((4 * SEL, 128), BF)),
        (rank, hold(normed.reshape(NT, ROWS, D)), hold(hidden)),
        smem=(0,),
        hbm=(0, 1, 2),
        after=(part,),
        flops=2 * 100_000_000,
        size=2 << 20,
    )
    unit, enorm, spread, four = call(
        embed_body,
        (sds((ROWS, D), F32), sds((ROWS, 128), F32), blocks, sds((4, ROWS, D), BF)),
        (rank, images, tensor_all(part), texts, dp(texts, 4), dp(texts, 8), dp(texts, 12)),
        smem=(0,),
        hbm=(0, 1, 2, 3),
        after=(n_own,),
    )
    t_own = [four, dp(four, 2), dp(four, 16), dp(four, 18)]
    t_oth = [dp(x, 1) for x in t_own]
    unit_b = tensor_all(spread)
    du, c_own, c_oth, again = call(
        pairs_body,
        (blocks, sds((IMG, 256), BF), sds((IMG, 256), BF), blocks),
        (rank, log_scale, bias, unit_b, hold(four), *t_own[1:], *t_oth),
        smem=(0, 1, 2),
        hbm=(0, 1, 2, 3),
        flops=2 * 150_000_000,
        size=2 << 20,
    )
    u_got = dp(again, 1)
    c_got = dp(c_oth, 1)
    sixty = sds((4 * ROWS, D), BF)
    keep, *sent = call(
        text_grad_body,
        (sds((4 * ROWS, D), F32), sixty, sixty, sixty),
        (log_scale, hold(c_own), unit_b, c_got, u_got),
        smem=(0,),
        hbm=(0, 1, 2, 3),
        flops=2 * 75_000_000,
        size=2 << 20,
    )
    got = [dp(x, mask) for x, mask in zip(sent, (2, 16, 18))]
    n_core = dp(n_own, 1)
    n_x = dp(n_tox, 16)
    n_xc = dp(n_x, 1)
    de_rows, spread = call(
        embed_grad_body,
        (block, blocks),
        (tensor_all(du), unit, enorm),
        hbm=(0, 1),
        after=(keep,),
    )
    de = tensor_all(spread)

    operand = sds((3 * SEL, 128), BF)
    dpre, e_mine, e_own, e_tox, e_toxc = call(
        slope_body,
        (sds((IMG, FF_T), BF), sds((SEL, 128), BF), operand, operand, operand),
        (rank, de, hold(w_out), hold(slope)),
        smem=(0,),
        hbm=(1, 2, 3, 4),
        beside=(n_x,),
        flops=2 * 180_000_000,
        size=4 << 20,
    )
    e_x = dp(e_tox, 16)
    e_xc = dp(e_toxc, 17)
    e_core = dp(e_own, 1)
    dn, rest, *sent = call(
        dn_body,
        (blocks, sds((ROWS, D), F32), block, block, block),
        (dpre, w_in, keep, *got),
        hbm=(0, 1, 2, 3, 4),
        beside=(n_core, n_xc),
        flops=2 * 80_000_000,
        size=2 << 20,
    )
    dn = tensor_all(dn)
    got = [dp(x, mask) for x, mask in zip(sent, (4, 8, 12))]
    rows = call(
        image_body, block, (rank, dn, images, gain, de_rows), smem=(0,), hbm=(0,), beside=(e_core,)
    )
    payload = call(
        weights_body,
        sds((8, 40, D), BF),
        (n_mine, n_own, n_core, n_x, n_xc)
        + (hold(e_mine), hold(e_own), e_core, e_x, e_xc),
        hbm=(0,),
        after=(rows,),
        beside=got,
        flops=2 * 160_000_000,
        size=3 << 20,
    )
    total = lax.all_to_all(payload, "dp", 0, 0, tiled=True, axis_index_groups=groups)

    spread = [rows] + [swap(rows, "tensor", NT, k) for k in (1, 2, 4, 6)]
    spread += [swap(spread[1], "tensor", NT, k) for k in (2, 4, 6)]
    image_grad = call(place_body, sds((IMG, D), F32), (rank, *spread), smem=(0,))
    text_grad, in_grad, out_grad = call(
        final_body,
        (sds((ROWS, D), F32), sds((COLS, FF_T), F32), sds((COLS, FF_T), F32)),
        (total, texts, rest, *got),
    )
    return (image_grad, text_grad, in_grad, out_grad)


def solution(mesh):
    return jax.shard_map(
        local,
        mesh=mesh,
        in_specs=(
            P("dp", None),
            P(),
            P(None, "tensor"),
            P("tensor"),
            P("tensor", None),
            P(("dp", "tensor"), None),
            P(),
            P(),
        ),
        out_specs=(P("dp", None), P(("dp", "tensor"), None), P("dp", "tensor"), P("dp", "tensor")),
        check_vma=False,
    )
```

```python
import jax
import jax.numpy as jnp
from jax import lax
from jax.experimental import pallas as pl
from jax.experimental.pallas import tpu as pltpu
from jax.sharding import PartitionSpec as P

F32 = jnp.float32
BF = jnp.bfloat16
I32 = jnp.int32
D = 1152
FF_T = 538
NT = 8
ROWS = 16
COLS = 36
IMG = 128
SEL = 320
LANES = 640
OUT_AT = 576
ROOT = 0.7978845608028654


def dot(a, b, ca=1, cb=0):
    return lax.dot_general(a, b, (((ca,), (cb,)), ((), ())), preferred_element_type=F32)


def swap(x, axis, n, mask):
    return lax.ppermute(x, axis, [(i, i ^ mask) for i in range(n)])


def sds(shape, dtype):
    return jax.ShapeDtypeStruct(shape, dtype)


def hold(x):
    return pltpu.with_memory_space_constraint(x, pltpu.HBM)


def call(body, outs, args, scratch=(), smem=(), after=(), beside=(), hbm=(), flops=0, size=1 << 20):
    single = not isinstance(outs, (tuple, list))
    outs = (outs,) if single else tuple(outs)
    vm = pl.BlockSpec(memory_space=pltpu.VMEM)
    sm = pl.BlockSpec(memory_space=pltpu.SMEM)
    some = pl.BlockSpec(memory_space=pl.ANY)
    far = pl.BlockSpec(memory_space=pltpu.HBM)
    order = [hold(x) for x in after] + list(beside)
    n_in, n_after, n_out, n_far = len(args), len(order), len(outs), len(hbm)

    def kernel(*refs):
        ins = refs[:n_in]
        results = list(refs[n_in + n_after : n_in + n_after + n_out])
        rest = refs[n_in + n_after + n_out :]
        near, sems, own = rest[:n_far], rest[n_far : 2 * n_far], rest[2 * n_far :]
        copies = []
        for ref, at, sem in zip(near, hbm, sems):
            copies.append(pltpu.make_async_copy(ref, results[at], sem))
            results[at] = ref
        body(*ins, *results, *own)
        for copy in copies:
            copy.start()
        for copy in copies:
            copy.wait()

    got = pl.pallas_call(
        kernel,
        out_shape=tuple(
            pltpu.HBM(o.shape, o.dtype) if i in hbm else o for i, o in enumerate(outs)
        ),
        in_specs=[sm if i in smem else vm for i in range(n_in)] + [some] * n_after,
        out_specs=tuple(far if i in hbm else vm for i in range(n_out)),
        scratch_shapes=[pltpu.VMEM(outs[i].shape, outs[i].dtype) for i in hbm]
        + [pltpu.SemaphoreType.DMA(()) for _ in hbm]
        + list(scratch),
        compiler_params=pltpu.CompilerParams(vmem_limit_bytes=24 << 20),
        cost_estimate=pl.CostEstimate(flops=flops, bytes_accessed=size, transcendentals=0),
    )(*args, *order)
    return got[0] if single else got


def text_unit(tf):
    tnorm = jnp.sqrt(jnp.sum(tf * tf, axis=-1, keepdims=True) + 1e-06)
    return tf / tnorm, tnorm


def text_body(mine, *refs):
    out = refs[3]
    for k, ref in enumerate((mine,) + refs[:3]):
        out[k] = text_unit(ref[...].astype(F32))[0].astype(BF)


def layer_stats(xf):
    centered = xf - jnp.mean(xf, axis=-1, keepdims=True)
    sd = jnp.sqrt(jnp.mean(centered * centered, axis=-1, keepdims=True) + 1e-06)
    return centered / sd, sd


def forward_body(images, gain, w_in, b_in, w_out, normed, hidden, slope, part, *scratch):
    v_images, v_in, v_out, v_normed, v_hidden, v_slope, v_part, sem = scratch

    def move(src, dst, k):
        copy = pltpu.make_async_copy(src, dst, sem.at[k])
        copy.start()
        return copy

    get_images = move(images, v_images, 0)
    get_in = move(w_in, v_in, 1)
    get_out = move(w_out, v_out, 2)
    get_images.wait()
    xhat, _ = layer_stats(v_images[...].astype(F32))
    normed_b = (xhat * gain[...].reshape(1, D)).astype(BF)
    v_normed[...] = normed_b
    put_normed = move(v_normed, normed, 3)
    get_in.wait()
    pre = dot(normed_b, v_in[...], 1, 1) + b_in[...].reshape(1, FF_T)
    square = pre * pre
    th = jnp.tanh(ROOT * (pre + 0.044715 * (square * pre)))
    cdf = 0.5 * (1.0 + th)
    hidden_b = (pre * cdf).astype(BF)
    v_hidden[...] = hidden_b
    put_hidden = move(v_hidden, hidden, 4)
    v_slope[...] = cdf + 0.5 * pre * (1.0 - th * th) * (ROOT * (1.0 + 0.134145 * square))
    put_slope = move(v_slope, slope, 6)
    get_out.wait()
    v_part[...] = dot(hidden_b, v_out[...]).astype(BF).reshape(NT, ROWS, D)
    put_part = move(v_part, part, 5)
    for copy in (put_normed, put_hidden, put_part, put_slope):
        copy.wait()


def forward(images, gain, w_in, b_in, w_out):
    far = pl.BlockSpec(memory_space=pltpu.HBM)
    near = pl.BlockSpec(memory_space=pltpu.VMEM)

    shapes = (
        ((IMG, D), BF),
        ((IMG, FF_T), BF),
        ((IMG, FF_T), F32),
        ((NT, ROWS, D), BF),
    )
    return pl.pallas_call(
        forward_body,
        out_shape=tuple(pltpu.HBM(*shape) for shape in shapes),
        in_specs=[far, near, far, near, far],
        out_specs=(far,) * 4,
        scratch_shapes=[
            pltpu.VMEM((IMG, D), BF),
            pltpu.VMEM((FF_T, D), BF),
            pltpu.VMEM((FF_T, D), BF),
        ]
        + [pltpu.VMEM(*shape) for shape in shapes]
        + [pltpu.SemaphoreType.DMA((7,))],
        compiler_params=pltpu.CompilerParams(vmem_limit_bytes=24 << 20),
        cost_estimate=pl.CostEstimate(
            flops=2 * 160_000_000, bytes_accessed=4 << 20, transcendentals=0
        ),
    )(hold(images), hold(gain), hold(w_in), hold(b_in), hold(w_out))


def embed_body(rank, images, got, t_a, t_b, t_c, t_d, unit, enorm, spread, four):
    text_body(t_a, t_b, t_c, t_d, four)
    at = pl.multiple_of(rank[0] * ROWS, ROWS)
    embed = images[pl.ds(at, ROWS), :].astype(F32)
    embed = embed + jnp.sum(got[...].astype(F32), axis=0)
    norm = jnp.sqrt(jnp.sum(embed * embed, axis=-1, keepdims=True) + 1e-06)
    value = embed / norm
    unit[...] = value
    enorm[...] = jnp.broadcast_to(norm, (ROWS, 128))
    value = value.astype(BF)
    for k in range(NT):
        spread[k] = value


def pairs_body(rank, log_scale, bias, unit, *refs):
    du, c_own, c_oth, again = refs[8:]
    again[...] = unit[...]
    scale = jnp.exp(jnp.full((1, 1), log_scale[0], F32))
    u = unit[...].reshape(IMG, D)
    total = None
    for half, out in ((0, c_own), (4, c_oth)):
        texts = jnp.concatenate([ref[...].reshape(64, D) for ref in refs[half : half + 4]], axis=0)
        coef = jax.nn.sigmoid(scale * dot(u, texts, 1, 1) + bias[0])
        if half == 0:
            row = lax.broadcasted_iota(I32, (IMG, 256), 0) - rank[0] * ROWS
            col = lax.broadcasted_iota(I32, (IMG, 256), 1)
            coef = coef - jnp.where((row == col) & (col < ROWS), 1.0, 0.0)
        coef = coef.astype(BF)
        out[...] = coef
        part = dot(coef, texts)
        total = part if half == 0 else total + part
    du[...] = (scale * total).astype(BF).reshape(NT, ROWS, D)


def text_grad_body(log_scale, c_mine, u_mine, c_got, u_got, keep, *sent):
    scale = jnp.exp(jnp.full((1, 1), log_scale[0], F32))
    dw = dot(c_mine[...], u_mine[...].reshape(IMG, D), 0, 0)
    dw = scale * (dw + dot(c_got[...], u_got[...].reshape(IMG, D), 0, 0))
    keep[...] = dw[:64]
    for k in range(3):
        sent[k][...] = dw[64 * (k + 1) : 64 * (k + 2)].astype(BF)


def text_fold_body(keep, a, b, c, rest, *sent):
    dw = keep[...] + a[...].astype(F32) + b[...].astype(F32) + c[...].astype(F32)
    rest[...] = dw[:ROWS]
    for k in range(3):
        sent[k][...] = dw[ROWS * (k + 1) : ROWS * (k + 2)].astype(BF)


def embed_grad_body(got, unit, enorm, rows, spread):
    du = jnp.sum(got[...].astype(F32), axis=0)
    u = unit[...]
    de = (du - u * jnp.sum(u * du, axis=-1, keepdims=True)) / enorm[:, :1]
    de = de.astype(BF)
    rows[...] = de
    for k in range(NT):
        spread[k] = de


def slope_body(rank, de, w_out, slope, dpre, *sent):
    value = dot(de[...].reshape(IMG, D), w_out[...], 1, 1) * slope[...]
    dpre[...] = value.astype(BF)
    pack_body(rank, de, dpre, *sent)


def dn_body(dpre, w_in, keep, t_a, t_b, t_c, dn, rest, *sent):
    dn[...] = dot(dpre[...], w_in[...]).astype(BF).reshape(NT, ROWS, D)
    text_fold_body(keep, t_a, t_b, t_c, rest, *sent)


def pack(rank, left, right, lefts, rights):
    r = lax.broadcasted_iota(I32, (SEL, 1), 0)
    block = (r * 52429) >> 21
    place = r - block * 40
    base = jnp.where(place < COLS, block * 72 + place, -4096)
    diff = lax.broadcasted_iota(I32, (SEL, LANES), 1) - base
    for ref, at, x_flip, c_flip in lefts:
        x, c = rank[2] ^ x_flip, rank[1] ^ c_flip
        window = pl.ds(pl.multiple_of(x * 512, 512), LANES)
        one = jnp.where(diff == x * 64 + c * COLS, 1.0, 0.0).astype(BF)
        ref[at : at + SEL] = dot(one, left[:, :, window].reshape(IMG, LANES), 1, 1).astype(BF)
    wide = jnp.concatenate([right[...].astype(F32), jnp.zeros((IMG, LANES - FF_T), F32)], axis=1)
    wide = wide.astype(BF)
    for k in range(5):
        for ref, at in rights:
            ref[at + k * 128 : at + (k + 1) * 128] = wide[:, k * 128 : (k + 1) * 128]


def pack_relay_body(rank, left, right, mine, to_core, to_x):
    lefts = ((mine, 0, 0, 0), (to_core, 0, 0, 1), (to_x, 0, 1, 0), (to_x, SEL, 1, 1))
    pack(rank, left, right, lefts, ((to_core, SEL), (to_x, 2 * SEL)))


def pack_body(rank, left, right, mine, to_core, to_x, to_both):
    lefts = ((to_x, 0, 1, 0), (to_both, 0, 1, 1), (mine, 0, 0, 0), (to_core, 0, 0, 1))
    pack(rank, left, right, lefts, ((to_core, SEL), (to_x, SEL), (to_both, SEL)))


def weights_body(*refs):
    n_mine, n_own, n_core, n_x, n_xc = refs[:5]
    e_mine, e_own, e_core, e_x, e_xc = refs[5:10]
    out = refs[10]

    def left(*parts):
        return jnp.concatenate([ref[at : at + SEL] for ref, at in parts], axis=1)

    def right(*parts):
        rows = []
        for ref, at in parts:
            chunks = [ref[at + k * 128 : at + (k + 1) * 128] for k in range(5)]
            rows.append(jnp.concatenate(chunks, axis=1))
        return jnp.concatenate(rows, axis=0)

    in_part = dot(
        left((n_mine, 0), (n_core, 0), (n_x, 0), (n_xc, SEL)),
        right((e_own, SEL), (e_core, SEL), (e_x, SEL), (e_xc, SEL)),
    )
    out_part = dot(
        left((e_mine, 0), (e_core, 0), (e_x, 0), (e_xc, 0)),
        right((n_own, SEL), (n_core, SEL), (n_x, 2 * SEL), (n_xc, 2 * SEL)),
    )
    both = jnp.concatenate([in_part[:, :OUT_AT], out_part[:, :OUT_AT]], axis=1)
    for k in range(8):
        out[k] = both[k * 40 : (k + 1) * 40].astype(BF)


def image_body(rank, got, images, gain, de_rows, rows):
    dn = jnp.sum(got[...].astype(F32), axis=0)
    at = pl.multiple_of(rank[0] * ROWS, ROWS)
    xhat, sd = layer_stats(images[pl.ds(at, ROWS), :].astype(F32))
    dxh = dn * gain[...].reshape(1, D)
    grad = (
        dxh
        - jnp.mean(dxh, axis=-1, keepdims=True)
        - xhat * jnp.mean(dxh * xhat, axis=-1, keepdims=True)
    ) / sd
    rows[...] = (de_rows[...].astype(F32) + grad).astype(BF)


def place_body(rank, *refs):
    out = refs[NT]
    for ref, k in zip(refs[:NT], (0, 1, 2, 4, 6, 3, 5, 7)):
        at = pl.multiple_of((rank[0] ^ k) * ROWS, ROWS)
        out[pl.ds(at, ROWS), :] = ref[...].astype(F32)


def final_body(got, texts, rest, a, b, c, text_grad, in_grad, out_grad):
    total = got[0].astype(F32)
    for k in range(1, 8):
        total = total + got[k].astype(F32)
    in_grad[...] = total[:COLS, 0:FF_T]
    out_grad[...] = total[:COLS, OUT_AT : OUT_AT + FF_T]
    dw = rest[...] + a[...].astype(F32) + b[...].astype(F32) + c[...].astype(F32)
    tunit, tnorm = text_unit(texts[...].astype(F32))
    text_grad[...] = (dw - tunit * jnp.sum(tunit * dw, axis=-1, keepdims=True)) / tnorm


def local(images, gain, w_in, b_in, w_out, texts, log_scale, bias):
    rank_d = lax.axis_index("dp")
    rank_t = lax.axis_index("tensor")
    rank = jnp.stack([rank_t, rank_d % 2, rank_d // 16]).astype(I32)
    w_in = w_in.T
    block = sds((ROWS, D), BF)
    blocks = sds((NT, ROWS, D), BF)
    groups = [[x * 16 + k * 2 + c for k in range(8)] for x in range(2) for c in range(2)]

    def tensor_all(x):
        return lax.all_to_all(x, "tensor", 0, 0, tiled=True)

    def dp(x, mask):
        return swap(x, "dp", 32, mask)

    normed, hidden, slope, part = forward(images, gain, w_in, b_in, w_out)
    n_mine, n_own, n_tox = call(
        pack_relay_body,
        (sds((SEL, 128), BF), sds((3 * SEL, 128), BF), sds((4 * SEL, 128), BF)),
        (rank, hold(normed.reshape(NT, ROWS, D)), hold(hidden)),
        smem=(0,),
        hbm=(0, 1, 2),
        after=(part,),
        flops=2 * 100_000_000,
        size=2 << 20,
    )
    unit, enorm, spread, four = call(
        embed_body,
        (sds((ROWS, D), F32), sds((ROWS, 128), F32), blocks, sds((4, ROWS, D), BF)),
        (rank, images, tensor_all(part), texts, dp(texts, 8), dp(texts, 4), dp(texts, 12)),
        smem=(0,),
        hbm=(0, 1, 2, 3),
        after=(n_own,),
    )
    t_own = [four, dp(four, 18), dp(four, 16), dp(four, 2)]
    t_oth = [dp(x, 1) for x in t_own]
    unit_b = tensor_all(spread)
    du, c_own, c_oth, again = call(
        pairs_body,
        (blocks, sds((IMG, 256), BF), sds((IMG, 256), BF), blocks),
        (rank, log_scale, bias, unit_b, hold(four), *t_own[1:], *t_oth),
        smem=(0, 1, 2),
        hbm=(0, 1, 2, 3),
        flops=2 * 150_000_000,
        size=2 << 20,
    )
    u_got = dp(again, 1)
    c_got = dp(c_oth, 1)
    sixty = sds((4 * ROWS, D), BF)
    keep, *sent = call(
        text_grad_body,
        (sds((4 * ROWS, D), F32), sixty, sixty, sixty),
        (log_scale, hold(c_own), unit_b, c_got, u_got),
        smem=(0,),
        hbm=(0, 1, 2, 3),
        flops=2 * 75_000_000,
        size=2 << 20,
    )
    got = [dp(x, mask) for x, mask in zip(sent, (18, 16, 2))]
    n_core = dp(n_own, 1)
    n_x = dp(n_tox, 16)
    n_xc = dp(n_x, 1)
    de_rows, spread = call(
        embed_grad_body,
        (block, blocks),
        (tensor_all(du), unit, enorm),
        hbm=(0, 1),
        after=(keep,),
    )
    de = tensor_all(spread)

    operand = sds((3 * SEL, 128), BF)
    dpre, e_mine, e_own, e_tox, e_toxc = call(
        slope_body,
        (sds((IMG, FF_T), BF), sds((SEL, 128), BF), operand, operand, operand),
        (rank, de, hold(w_out), hold(slope)),
        smem=(0,),
        hbm=(1, 2, 3, 4),
        beside=(n_x,),
        flops=2 * 180_000_000,
        size=4 << 20,
    )
    e_x = dp(e_tox, 16)
    e_xc = dp(e_toxc, 17)
    e_core = dp(e_own, 1)
    dn, rest, *sent = call(
        dn_body,
        (blocks, sds((ROWS, D), F32), block, block, block),
        (dpre, w_in, keep, *got),
        hbm=(0, 1, 2, 3, 4),
        beside=(n_core, n_xc),
        flops=2 * 80_000_000,
        size=2 << 20,
    )
    dn = tensor_all(dn)
    got = [dp(x, mask) for x, mask in zip(sent, (8, 4, 12))]
    rows = call(
        image_body, block, (rank, dn, images, gain, de_rows), smem=(0,), hbm=(0,), beside=(e_core,)
    )
    payload = call(
        weights_body,
        sds((8, 40, D), BF),
        (n_mine, n_own, n_core, n_x, n_xc)
        + (hold(e_mine), hold(e_own), e_core, e_x, e_xc),
        hbm=(0,),
        after=(rows,),
        beside=got,
        flops=2 * 160_000_000,
        size=3 << 20,
    )
    total = lax.all_to_all(payload, "dp", 0, 0, tiled=True, axis_index_groups=groups)

    spread = [rows] + [swap(rows, "tensor", NT, k) for k in (1, 2, 4, 6)]
    spread += [swap(spread[1], "tensor", NT, k) for k in (2, 4, 6)]
    image_grad = call(place_body, sds((IMG, D), F32), (rank, *spread), smem=(0,))
    text_grad, in_grad, out_grad = call(
        final_body,
        (sds((ROWS, D), F32), sds((COLS, FF_T), F32), sds((COLS, FF_T), F32)),
        (total, texts, rest, *got),
    )
    return (image_grad, text_grad, in_grad, out_grad)


def solution(mesh):
    return jax.shard_map(
        local,
        mesh=mesh,
        in_specs=(
            P("dp", None),
            P(),
            P(None, "tensor"),
            P("tensor"),
            P("tensor", None),
            P(("dp", "tensor"), None),
            P(),
            P(),
        ),
        out_specs=(P("dp", None), P(("dp", "tensor"), None), P("dp", "tensor"), P("dp", "tensor")),
        check_vma=False,
    )
```

```python
import jax
import jax.numpy as jnp
from jax import lax
from jax.experimental import pallas as pl
from jax.experimental.pallas import tpu as pltpu
from jax.sharding import PartitionSpec as P

F32 = jnp.float32
BF = jnp.bfloat16
I32 = jnp.int32
D = 1152
FF_T = 538
NT = 8
ROWS = 16
COLS = 36
IMG = 128
SEL = 320
LANES = 640
OUT_AT = 576
ROOT = 0.7978845608028654


def dot(a, b, ca=1, cb=0):
    return lax.dot_general(a, b, (((ca,), (cb,)), ((), ())), preferred_element_type=F32)


def swap(x, axis, n, mask):
    return lax.ppermute(x, axis, [(i, i ^ mask) for i in range(n)])


def sds(shape, dtype):
    return jax.ShapeDtypeStruct(shape, dtype)


def hold(x):
    return pltpu.with_memory_space_constraint(x, pltpu.HBM)


def call(body, outs, args, scratch=(), smem=(), after=(), beside=(), hbm=(), flops=0, size=1 << 20):
    single = not isinstance(outs, (tuple, list))
    outs = (outs,) if single else tuple(outs)
    vm = pl.BlockSpec(memory_space=pltpu.VMEM)
    sm = pl.BlockSpec(memory_space=pltpu.SMEM)
    some = pl.BlockSpec(memory_space=pl.ANY)
    far = pl.BlockSpec(memory_space=pltpu.HBM)
    order = [hold(x) for x in after] + list(beside)
    n_in, n_after, n_out, n_far = len(args), len(order), len(outs), len(hbm)

    def kernel(*refs):
        ins = refs[:n_in]
        results = list(refs[n_in + n_after : n_in + n_after + n_out])
        rest = refs[n_in + n_after + n_out :]
        near, sems, own = rest[:n_far], rest[n_far : 2 * n_far], rest[2 * n_far :]
        copies = []
        for ref, at, sem in zip(near, hbm, sems):
            copies.append(pltpu.make_async_copy(ref, results[at], sem))
            results[at] = ref
        body(*ins, *results, *own)
        for copy in copies:
            copy.start()
        for copy in copies:
            copy.wait()

    got = pl.pallas_call(
        kernel,
        out_shape=tuple(
            pltpu.HBM(o.shape, o.dtype) if i in hbm else o for i, o in enumerate(outs)
        ),
        in_specs=[sm if i in smem else vm for i in range(n_in)] + [some] * n_after,
        out_specs=tuple(far if i in hbm else vm for i in range(n_out)),
        scratch_shapes=[pltpu.VMEM(outs[i].shape, outs[i].dtype) for i in hbm]
        + [pltpu.SemaphoreType.DMA(()) for _ in hbm]
        + list(scratch),
        compiler_params=pltpu.CompilerParams(vmem_limit_bytes=24 << 20),
        cost_estimate=pl.CostEstimate(flops=flops, bytes_accessed=size, transcendentals=0),
    )(*args, *order)
    return got[0] if single else got


def text_unit(tf):
    tnorm = jnp.sqrt(jnp.sum(tf * tf, axis=-1, keepdims=True) + 1e-06)
    return tf / tnorm, tnorm


def text_body(mine, *refs):
    out = refs[3]
    for k, ref in enumerate((mine,) + refs[:3]):
        out[k] = text_unit(ref[...].astype(F32))[0].astype(BF)


def layer_stats(xf):
    centered = xf - jnp.mean(xf, axis=-1, keepdims=True)
    sd = jnp.sqrt(jnp.mean(centered * centered, axis=-1, keepdims=True) + 1e-06)
    return centered / sd, sd


def forward_body(images, gain, w_in, b_in, w_out, normed, hidden, slope, part, *scratch):
    v_images, v_in, v_out, v_normed, v_hidden, v_slope, v_part, sem = scratch

    def move(src, dst, k):
        copy = pltpu.make_async_copy(src, dst, sem.at[k])
        copy.start()
        return copy

    get_images = move(images, v_images, 0)
    get_in = move(w_in, v_in, 1)
    get_out = move(w_out, v_out, 2)
    get_images.wait()
    xhat, _ = layer_stats(v_images[...].astype(F32))
    normed_b = (xhat * gain[...].reshape(1, D)).astype(BF)
    v_normed[...] = normed_b
    put_normed = move(v_normed, normed, 3)
    get_in.wait()
    pre = dot(normed_b, v_in[...], 1, 1) + b_in[...].reshape(1, FF_T)
    square = pre * pre
    th = jnp.tanh(ROOT * (pre + 0.044715 * (square * pre)))
    cdf = 0.5 * (1.0 + th)
    hidden_b = (pre * cdf).astype(BF)
    v_hidden[...] = hidden_b
    put_hidden = move(v_hidden, hidden, 4)
    v_slope[...] = cdf + 0.5 * pre * (1.0 - th * th) * (ROOT * (1.0 + 0.134145 * square))
    put_slope = move(v_slope, slope, 6)
    get_out.wait()
    v_part[...] = dot(hidden_b, v_out[...]).astype(BF).reshape(NT, ROWS, D)
    put_part = move(v_part, part, 5)
    for copy in (put_normed, put_hidden, put_part, put_slope):
        copy.wait()


def forward(images, gain, w_in, b_in, w_out):
    far = pl.BlockSpec(memory_space=pltpu.HBM)
    near = pl.BlockSpec(memory_space=pltpu.VMEM)

    shapes = (
        ((IMG, D), BF),
        ((IMG, FF_T), BF),
        ((IMG, FF_T), F32),
        ((NT, ROWS, D), BF),
    )
    return pl.pallas_call(
        forward_body,
        out_shape=tuple(pltpu.HBM(*shape) for shape in shapes),
        in_specs=[far, near, far, near, far],
        out_specs=(far,) * 4,
        scratch_shapes=[
            pltpu.VMEM((IMG, D), BF),
            pltpu.VMEM((FF_T, D), BF),
            pltpu.VMEM((FF_T, D), BF),
        ]
        + [pltpu.VMEM(*shape) for shape in shapes]
        + [pltpu.SemaphoreType.DMA((7,))],
        compiler_params=pltpu.CompilerParams(vmem_limit_bytes=24 << 20),
        cost_estimate=pl.CostEstimate(
            flops=2 * 160_000_000, bytes_accessed=4 << 20, transcendentals=0
        ),
    )(hold(images), hold(gain), hold(w_in), hold(b_in), hold(w_out))


def embed_body(rank, images, got, t_a, t_b, t_c, t_d, unit, enorm, spread, four):
    text_body(t_a, t_b, t_c, t_d, four)
    at = pl.multiple_of(rank[0] * ROWS, ROWS)
    embed = images[pl.ds(at, ROWS), :].astype(F32)
    embed = embed + jnp.sum(got[...].astype(F32), axis=0)
    norm = jnp.sqrt(jnp.sum(embed * embed, axis=-1, keepdims=True) + 1e-06)
    value = embed / norm
    unit[...] = value
    enorm[...] = jnp.broadcast_to(norm, (ROWS, 128))
    value = value.astype(BF)
    for k in range(NT):
        spread[k] = value


def pairs_body(rank, log_scale, bias, unit, *refs):
    du, c_own, c_oth, again = refs[8:]
    again[...] = unit[...]
    scale = jnp.exp(jnp.full((1, 1), log_scale[0], F32))
    u = unit[...].reshape(IMG, D)
    total = None
    for half, out in ((0, c_own), (4, c_oth)):
        texts = jnp.concatenate([ref[...].reshape(64, D) for ref in refs[half : half + 4]], axis=0)
        coef = jax.nn.sigmoid(scale * dot(u, texts, 1, 1) + bias[0])
        if half == 0:
            row = lax.broadcasted_iota(I32, (IMG, 256), 0) - rank[0] * ROWS
            col = lax.broadcasted_iota(I32, (IMG, 256), 1)
            coef = coef - jnp.where((row == col) & (col < ROWS), 1.0, 0.0)
        coef = coef.astype(BF)
        out[...] = coef
        part = dot(coef, texts)
        total = part if half == 0 else total + part
    du[...] = (scale * total).astype(BF).reshape(NT, ROWS, D)


def text_grad_body(log_scale, c_mine, u_mine, c_got, u_got, keep, *sent):
    scale = jnp.exp(jnp.full((1, 1), log_scale[0], F32))
    dw = dot(c_mine[...], u_mine[...].reshape(IMG, D), 0, 0)
    dw = scale * (dw + dot(c_got[...], u_got[...].reshape(IMG, D), 0, 0))
    keep[...] = dw[:64]
    for k in range(3):
        sent[k][...] = dw[64 * (k + 1) : 64 * (k + 2)].astype(BF)


def text_fold_body(keep, a, b, c, rest, *sent):
    dw = keep[...] + a[...].astype(F32) + b[...].astype(F32) + c[...].astype(F32)
    rest[...] = dw[:ROWS]
    for k in range(3):
        sent[k][...] = dw[ROWS * (k + 1) : ROWS * (k + 2)].astype(BF)


def embed_grad_body(got, unit, enorm, rows, spread):
    du = jnp.sum(got[...].astype(F32), axis=0)
    u = unit[...]
    de = (du - u * jnp.sum(u * du, axis=-1, keepdims=True)) / enorm[:, :1]
    de = de.astype(BF)
    rows[...] = de
    for k in range(NT):
        spread[k] = de


def slope_body(rank, de, w_out, slope, dpre, *sent):
    value = dot(de[...].reshape(IMG, D), w_out[...], 1, 1) * slope[...]
    dpre[...] = value.astype(BF)
    pack_body(rank, de, dpre, *sent)


def dn_body(dpre, w_in, keep, t_a, t_b, t_c, dn, rest, *sent):
    dn[...] = dot(dpre[...], w_in[...]).astype(BF).reshape(NT, ROWS, D)
    text_fold_body(keep, t_a, t_b, t_c, rest, *sent)


def pack(rank, left, right, lefts, rights):
    r = lax.broadcasted_iota(I32, (SEL, 1), 0)
    block = (r * 52429) >> 21
    place = r - block * 40
    base = jnp.where(place < COLS, block * 72 + place, -4096)
    diff = lax.broadcasted_iota(I32, (SEL, LANES), 1) - base
    for ref, at, x_flip, c_flip in lefts:
        x, c = rank[2] ^ x_flip, rank[1] ^ c_flip
        window = pl.ds(pl.multiple_of(x * 512, 512), LANES)
        one = jnp.where(diff == x * 64 + c * COLS, 1.0, 0.0).astype(BF)
        ref[at : at + SEL] = dot(one, left[:, :, window].reshape(IMG, LANES), 1, 1).astype(BF)
    wide = jnp.concatenate([right[...].astype(F32), jnp.zeros((IMG, LANES - FF_T), F32)], axis=1)
    wide = wide.astype(BF)
    for k in range(5):
        for ref, at in rights:
            ref[at + k * 128 : at + (k + 1) * 128] = wide[:, k * 128 : (k + 1) * 128]


def pack_relay_body(rank, left, right, mine, to_core, to_x):
    lefts = ((mine, 0, 0, 0), (to_core, 0, 0, 1), (to_x, 0, 1, 0), (to_x, SEL, 1, 1))
    pack(rank, left, right, lefts, ((to_core, SEL), (to_x, 2 * SEL)))


def pack_body(rank, left, right, mine, to_core, to_x, to_both):
    lefts = ((to_x, 0, 1, 0), (to_both, 0, 1, 1), (mine, 0, 0, 0), (to_core, 0, 0, 1))
    pack(rank, left, right, lefts, ((to_core, SEL), (to_x, SEL), (to_both, SEL)))


def weights_body(*refs):
    n_mine, n_own, n_core, n_x, n_xc = refs[:5]
    e_mine, e_own, e_core, e_x, e_xc = refs[5:10]
    out = refs[10]

    def left(*parts):
        return jnp.concatenate([ref[at : at + SEL] for ref, at in parts], axis=1)

    def right(*parts):
        rows = []
        for ref, at in parts:
            chunks = [ref[at + k * 128 : at + (k + 1) * 128] for k in range(5)]
            rows.append(jnp.concatenate(chunks, axis=1))
        return jnp.concatenate(rows, axis=0)

    in_part = dot(
        left((n_mine, 0), (n_core, 0), (n_x, 0), (n_xc, SEL)),
        right((e_own, SEL), (e_core, SEL), (e_x, SEL), (e_xc, SEL)),
    )
    out_part = dot(
        left((e_mine, 0), (e_core, 0), (e_x, 0), (e_xc, 0)),
        right((n_own, SEL), (n_core, SEL), (n_x, 2 * SEL), (n_xc, 2 * SEL)),
    )
    both = jnp.concatenate([in_part[:, :OUT_AT], out_part[:, :OUT_AT]], axis=1)
    for k in range(8):
        out[k] = both[k * 40 : (k + 1) * 40].astype(BF)


def image_body(rank, got, images, gain, de_rows, rows):
    dn = jnp.sum(got[...].astype(F32), axis=0)
    at = pl.multiple_of(rank[0] * ROWS, ROWS)
    xhat, sd = layer_stats(images[pl.ds(at, ROWS), :].astype(F32))
    dxh = dn * gain[...].reshape(1, D)
    grad = (
        dxh
        - jnp.mean(dxh, axis=-1, keepdims=True)
        - xhat * jnp.mean(dxh * xhat, axis=-1, keepdims=True)
    ) / sd
    rows[...] = (de_rows[...].astype(F32) + grad).astype(BF)


def place_body(rank, *refs):
    out = refs[NT]
    for ref, k in zip(refs[:NT], (0, 1, 2, 4, 6, 3, 5, 7)):
        at = pl.multiple_of((rank[0] ^ k) * ROWS, ROWS)
        out[pl.ds(at, ROWS), :] = ref[...].astype(F32)


def final_body(got, texts, rest, a, b, c, text_grad, in_grad, out_grad):
    total = got[0].astype(F32)
    for k in range(1, 8):
        total = total + got[k].astype(F32)
    in_grad[...] = total[:COLS, 0:FF_T]
    out_grad[...] = total[:COLS, OUT_AT : OUT_AT + FF_T]
    dw = rest[...] + a[...].astype(F32) + b[...].astype(F32) + c[...].astype(F32)
    tunit, tnorm = text_unit(texts[...].astype(F32))
    text_grad[...] = (dw - tunit * jnp.sum(tunit * dw, axis=-1, keepdims=True)) / tnorm


def local(images, gain, w_in, b_in, w_out, texts, log_scale, bias):
    rank_d = lax.axis_index("dp")
    rank_t = lax.axis_index("tensor")
    rank = jnp.stack([rank_t, rank_d % 2, rank_d // 16]).astype(I32)
    w_in = w_in.T
    block = sds((ROWS, D), BF)
    blocks = sds((NT, ROWS, D), BF)
    groups = [[x * 16 + k * 2 + c for k in range(8)] for x in range(2) for c in range(2)]

    def tensor_all(x):
        return lax.all_to_all(x, "tensor", 0, 0, tiled=True)

    def dp(x, mask):
        return swap(x, "dp", 32, mask)

    normed, hidden, slope, part = forward(images, gain, w_in, b_in, w_out)
    n_mine, n_own, n_tox = call(
        pack_relay_body,
        (sds((SEL, 128), BF), sds((3 * SEL, 128), BF), sds((4 * SEL, 128), BF)),
        (rank, hold(normed.reshape(NT, ROWS, D)), hold(hidden)),
        smem=(0,),
        hbm=(0, 1, 2),
        after=(part,),
        flops=2 * 100_000_000,
        size=2 << 20,
    )
    unit, enorm, spread, four = call(
        embed_body,
        (sds((ROWS, D), F32), sds((ROWS, 128), F32), blocks, sds((4, ROWS, D), BF)),
        (rank, images, tensor_all(part), texts, dp(texts, 8), dp(texts, 4), dp(texts, 12)),
        smem=(0,),
        hbm=(0, 1, 2, 3),
        after=(n_own,),
    )
    t_own = [four, dp(four, 2), dp(four, 16), dp(four, 18)]
    t_oth = [dp(x, 1) for x in t_own]
    unit_b = tensor_all(spread)
    du, c_own, c_oth, again = call(
        pairs_body,
        (blocks, sds((IMG, 256), BF), sds((IMG, 256), BF), blocks),
        (rank, log_scale, bias, unit_b, hold(four), *t_own[1:], *t_oth),
        smem=(0, 1, 2),
        hbm=(0, 1, 2, 3),
        flops=2 * 150_000_000,
        size=2 << 20,
    )
    u_got = dp(again, 1)
    c_got = dp(c_oth, 1)
    sixty = sds((4 * ROWS, D), BF)
    keep, *sent = call(
        text_grad_body,
        (sds((4 * ROWS, D), F32), sixty, sixty, sixty),
        (log_scale, hold(c_own), unit_b, c_got, u_got),
        smem=(0,),
        hbm=(0, 1, 2, 3),
        flops=2 * 75_000_000,
        size=2 << 20,
    )
    got = [dp(x, mask) for x, mask in zip(sent, (2, 16, 18))]
    n_core = dp(n_own, 1)
    n_x = dp(n_tox, 16)
    n_xc = dp(n_x, 1)
    de_rows, spread = call(
        embed_grad_body,
        (block, blocks),
        (tensor_all(du), unit, enorm),
        hbm=(0, 1),
        after=(keep,),
    )
    de = tensor_all(spread)

    operand = sds((3 * SEL, 128), BF)
    dpre, e_mine, e_own, e_tox, e_toxc = call(
        slope_body,
        (sds((IMG, FF_T), BF), sds((SEL, 128), BF), operand, operand, operand),
        (rank, de, hold(w_out), hold(slope)),
        smem=(0,),
        hbm=(1, 2, 3, 4),
        beside=(n_x,),
        flops=2 * 180_000_000,
        size=4 << 20,
    )
    e_x = dp(e_tox, 16)
    e_xc = dp(e_toxc, 17)
    e_core = dp(e_own, 1)
    dn, rest, *sent = call(
        dn_body,
        (blocks, sds((ROWS, D), F32), block, block, block),
        (dpre, w_in, keep, *got),
        hbm=(0, 1, 2, 3, 4),
        beside=(n_core, n_xc),
        flops=2 * 80_000_000,
        size=2 << 20,
    )
    dn = tensor_all(dn)
    got = [dp(x, mask) for x, mask in zip(sent, (8, 4, 12))]
    rows = call(
        image_body, block, (rank, dn, images, gain, de_rows), smem=(0,), hbm=(0,), beside=(e_core,)
    )
    payload = call(
        weights_body,
        sds((8, 40, D), BF),
        (n_mine, n_own, n_core, n_x, n_xc)
        + (hold(e_mine), hold(e_own), e_core, e_x, e_xc),
        hbm=(0,),
        after=(rows,),
        beside=got,
        flops=2 * 160_000_000,
        size=3 << 20,
    )
    total = lax.all_to_all(payload, "dp", 0, 0, tiled=True, axis_index_groups=groups)

    spread = [rows] + [swap(rows, "tensor", NT, k) for k in (1, 2, 4, 6)]
    spread += [swap(spread[1], "tensor", NT, k) for k in (2, 4, 6)]
    image_grad = call(place_body, sds((IMG, D), F32), (rank, *spread), smem=(0,))
    text_grad, in_grad, out_grad = call(
        final_body,
        (sds((ROWS, D), F32), sds((COLS, FF_T), F32), sds((COLS, FF_T), F32)),
        (total, texts, rest, *got),
    )
    return (image_grad, text_grad, in_grad, out_grad)


def solution(mesh):
    return jax.shard_map(
        local,
        mesh=mesh,
        in_specs=(
            P("dp", None),
            P(),
            P(None, "tensor"),
            P("tensor"),
            P("tensor", None),
            P(("dp", "tensor"), None),
            P(),
            P(),
        ),
        out_specs=(P("dp", None), P(("dp", "tensor"), None), P("dp", "tensor"), P("dp", "tensor")),
        check_vma=False,
    )
```
